512 devices in a mesh: dp: 8 (over x, y_hi), latent: 64 (over z, y_lo, core).
Axes of the slice: x: 4, y: 4 (y_hi: 2, y_lo: 2; y = y_hi * 2 + y_lo), z: 16, core: 2. Of those that a mesh axis runs over, the one named last changes fastest.
Arguments:
- resid: bfloat16 [1024, 3, 2304], P('dp', None, 'latent'), may hold values from -6 to 6
- target: bfloat16 [1024, 3, 2304], P('dp', None, 'latent'), may hold values from -6 to 6
- enc_weight: bfloat16 [24576, 2304], P('latent', 'dp'), may hold values from -0.125 to 0.125
- enc_bias: float32 [24576], P('latent'), may hold values from -0.6 to 0.6
- dec_weight: bfloat16 [24576, 3, 2304], P('latent', None, 'dp'), may hold values from -0.0625 to 0.0625
- source: int32 [24576], P('latent'), may hold values from 0 to 2, as said below
Outputs:
- loss: float32 [], replicated
- recon: bfloat16 [1024, 3, 2304], P('dp', None, 'latent')
- enc_grad: float32 [24576, 2304], P('latent', 'dp')
- bias_grad: float32 [24576], P('latent')
- dec_grad: float32 [24576, 3, 2304], P('latent', None, 'dp')
The draws below stay inside these ranges and needn't reach their ends.
Inputs may be any that keep to these rules, and one draw needn't show every extreme that they name: Each layer 0 to 2 is the source of exactly 8192 latents.
All inputs are finite; a program needn't handle non-finite values.
Results may differ from the reference program's by a relative error of at most 0.0095.
Values may be sent and summed in bfloat16 or wider, within the bound.
No kernel may reach another device: no remote copies, remote signals or barrier semaphores. Data moves between devices by JAX's collectives and lax.ppermute only.
A program may use at most 64 MiB of HBM per device.

```python
import jax
import jax.numpy as jnp
from jax import lax

D = 2304
F = 8192
LAYERS = 3
TOK_DEV = 128
TOKENS = 1024
LATENTS = 24576


def draw_source(key, part):
    key = jax.random.fold_in(key, 7)
    order = jax.random.permutation(key, LATENTS)
    return (order // F).astype(jnp.int32)


def level_of(key, shape, cuts, low, top_value):
    factor_of, own = 1.0, jax.random.fold_in(key, 6)
    for axis_at, parts in cuts:
        draws = jnp.exp(jax.random.uniform(jax.random.fold_in(own, axis_at), (parts,), jnp.float32, low / len(cuts), top_value / len(cuts)))
        factor_of = factor_of * jnp.repeat(draws, shape[axis_at] // parts).reshape([-1 if axis == axis_at else 1 for axis in range(len(shape))])
    return factor_of


def scatter_about(own_key, extent, spread, most, cuts=(), held_as=jnp.bfloat16):
    drawn = spread * jax.random.normal(own_key, extent, jnp.float32)
    if cuts:
        drawn = drawn * level_of(own_key, extent, cuts, -0.22, 0.18)
    return jnp.clip(drawn, -most, most).astype(held_as)


def setup_inputs(seed: int = 0) -> dict:
    seeds = jax.random.split(jax.random.key(seed), 7)
    resid = scatter_about(seeds[0], (TOKENS, LAYERS, D), 1.0, 6.0, ((0, 8), (2, 64)))
    target = scatter_about(seeds[1], (TOKENS, LAYERS, D), 1.0, 6.0, ((0, 8), (2, 64)))
    enc_weight = scatter_about(seeds[2], (LATENTS, D), D ** -0.5, 0.125, ((0, 64), (1, 8)))
    enc_bias = jnp.clip(jax.random.uniform(seeds[3], (LATENTS,), jnp.float32, -0.6, 0.6) * level_of(seeds[3], (LATENTS,), ((0, 64),), -0.4, 0.0), -0.6, 0.6)
    dec_weight = scatter_about(seeds[4], (LATENTS, LAYERS, D), F ** -0.5, 0.0625, ((0, 64), (2, 8)))
    source = draw_source(jax.random.fold_in(seeds[6], 71), 0)
    return dict(resid=resid, target=target, enc_weight=enc_weight, enc_bias=enc_bias, dec_weight=dec_weight, source=source)


sparsity_weight = 0.5
norm_epsilon = 1e-06

def reference(resid, target, enc_weight, enc_bias, dec_weight, source):
    layer_ids = jnp.arange(LAYERS, dtype=jnp.int32)
    pick = (source[:, None] == layer_ids[None, :]).astype(jnp.float32)
    reach = (source[:, None] <= layer_ids[None, :]).astype(jnp.float32)
    inputs = resid.astype(jnp.float32)
    every = jnp.einsum('tld,jd->tlj', inputs, enc_weight.astype(jnp.float32))
    pre = lax.optimization_barrier(jnp.sum(every * pick.T[None, :, :], axis=1)) + enc_bias[None, :]
    acts = jnp.maximum(pre, 0.0).astype(jnp.bfloat16)
    acts_wide = acts.astype(jnp.float32)
    decoder = dec_weight.astype(jnp.float32) * reach[:, :, None]
    norms = jnp.sqrt(lax.optimization_barrier(jnp.sum(decoder * decoder, axis=(1, 2))) + norm_epsilon)
    recon_sum = jnp.einsum('tj,jld->tld', acts_wide, decoder)
    error = recon_sum - target.astype(jnp.float32)
    loss = (jnp.sum(error * error) + sparsity_weight * jnp.sum(acts_wide * norms[None, :])) / TOK_DEV
    gout = (2.0 * error / TOK_DEV).astype(jnp.bfloat16).astype(jnp.float32)
    dacts = jnp.einsum('tld,jld->tj', gout, decoder) + sparsity_weight * norms[None, :] / TOK_DEV
    dpre = jnp.where(pre > 0, dacts, 0.0)
    dpre_low = dpre.astype(jnp.bfloat16).astype(jnp.float32)
    weighted = dpre_low[:, None, :] * pick.T[None, :, :]
    enc_grad = jnp.einsum('tlj,tld->jd', weighted, inputs)
    bias_grad = lax.optimization_barrier(jnp.sum(dpre, axis=0))
    colsum = lax.optimization_barrier(jnp.sum(acts_wide, axis=0))
    dec_grad = reach[:, :, None] * (jnp.einsum('tj,tld->jld', acts_wide, gout) + sparsity_weight * colsum[:, None, None] / TOK_DEV * decoder / norms[:, None, None])
    return (loss, recon_sum.astype(jnp.bfloat16), enc_grad, bias_grad, dec_grad)
```

```python
import jax
import jax.numpy as jnp
import numpy as np
from jax import lax
from jax.sharding import Mesh
from jax.sharding import PartitionSpec as P

LAYERS = 3
TOK_DEV = 128
SIZES = (4, 2, 16, 2, 2)
ALL = ("x", "yh", "z", "yl", "c")
DP = ("x", "yh")
LATENT = ("z", "yl", "c")
QUAD = ("yl", "c")
BLOCK = 112

sparsity_weight = 0.5
norm_epsilon = 1e-06
bf16, f32 = jnp.bfloat16, jnp.float32


def spread():
    pairs = []
    for a in range(8):
        for b in range(64):
            i, r = divmod(b, 8)
            pairs.append((a * 64 + b, i * 64 + ((a % 2) * 8 + r) * 4 + a // 2))
    return pairs


def pieces(value):
    high = lax.reduce_precision(value, 8, 7)
    middle = lax.reduce_precision(value - high, 8, 7)
    low = value - high - middle
    return [high.astype(bf16), middle.astype(bf16), low.astype(bf16)]


def share(block, axes, count):
    return lax.all_to_all(jnp.broadcast_to(block[None], (count, *block.shape)), axes, 0, 0)


def dot(spec, a, b):
    return jnp.einsum(spec, a, b, preferred_element_type=f32)


def on_device(resid, target, enc_weight, enc_bias, dec_weight, source):
    to = spread()
    back = [(d, s) for s, d in to]
    layer_ids = jnp.arange(LAYERS, dtype=jnp.int32)
    pick = source[None, :] == layer_ids[:, None]
    reach = source[None, :] <= layer_ids[:, None]

    both = jnp.stack([resid, target]).transpose(0, 2, 3, 1).reshape(2, 108, 128)
    both = jnp.pad(both, ((0, 0), (0, BLOCK - 108), (0, 0)))
    both = lax.ppermute(both, ALL, to)
    x_block, target_block = both[0], both[1]

    enc_t = enc_weight.T
    dec_t = jnp.where(reach[:, None, :], dec_weight.transpose(1, 2, 0), 0)
    square = jnp.sum(jnp.square(dec_t.astype(f32)), axis=(0, 1))
    dec_own = dec_t.reshape(3, 8, 36, 384).transpose(1, 0, 2, 3).reshape(8, 108, 384)
    dec_own = jnp.pad(dec_own, ((0, 0), (0, BLOCK - 108), (0, 0))).reshape(8 * BLOCK, 384)
    extra = jnp.stack([source.astype(bf16), *pieces(enc_bias), *pieces(square)])
    enc_own = jnp.concatenate([enc_t, jnp.pad(extra, ((0, 9), (0, 0)))])
    enc_quad = lax.all_gather(enc_own, QUAD)
    dec_quad = lax.all_gather(dec_own, QUAD)
    tail = enc_quad[:, 288:295].astype(f32)
    source_quad = tail[:, 0]
    bias_quad = (tail[:, 1] + tail[:, 2] + tail[:, 3]).reshape(1536)
    square_quad = (tail[:, 4] + tail[:, 5] + tail[:, 6]).reshape(1536)
    enc_rows = enc_quad[:, :288].reshape(4, 8, 1, 36, 384)
    pick_quad = source_quad[:, None, :] == layer_ids[None, :, None].astype(f32)
    enc_rows = jnp.where(pick_quad[:, None, :, None, :], enc_rows, 0).reshape(4, 8, 108, 384)
    enc_rows = jnp.pad(enc_rows, ((0, 0), (0, 0), (0, BLOCK - 108), (0, 0)))
    enc_rows = enc_rows.reshape(4, 8 * BLOCK, 384)

    x_quad = share(x_block, "z", 16).reshape(2, 8 * BLOCK, 128)
    partial = dot("akt,qkj->atqj", x_quad, enc_rows).reshape(8, 32, 1536)
    squares = jnp.broadcast_to(square_quad[None, None], (8, 8, 1536))
    summed = lax.all_to_all(jnp.concatenate([partial, squares], axis=1), DP, 0, 0).sum(0)
    pre = summed[:32] + bias_quad[None]
    norms = jnp.sqrt(summed[32] + norm_epsilon)
    acts = jnp.maximum(pre, 0.0).astype(bf16)
    sparsity = jnp.sum(acts.astype(f32) * norms[None])
    acts_quad = share(acts, DP, 8).reshape(2, 128, 4, 384)

    terms = dot("qkj,atqj->akt", dec_quad, acts_quad).astype(bf16).reshape(16, BLOCK, 128)
    recon_sum = lax.all_to_all(terms, "z", 0, 0).astype(f32).sum(0)
    recon = lax.ppermute(recon_sum.astype(bf16), ALL, back)
    recon = recon[:108].reshape(3, 36, 128).transpose(2, 0, 1)
    error = recon_sum - target_block.astype(f32)
    local_loss = jnp.sum(error * error) + sparsity_weight * sparsity
    gout = (2.0 * error / TOK_DEV).astype(bf16)
    loss_row = jnp.pad(jnp.stack(pieces(local_loss)), (0, 125))
    row_ids = lax.broadcasted_iota(jnp.int32, (BLOCK, 128), 0)
    gout = jnp.where(row_ids == 108, loss_row[None], gout)
    gout_all = share(gout, "z", 16)
    loss_z = jnp.sum(gout_all[:, 108, :3].astype(f32))
    gout_quad = gout_all.reshape(2, 8 * BLOCK, 128)

    slopes = dot("akt,qkj->atqj", gout_quad, dec_quad).astype(bf16).reshape(8, 32, 1536)
    slopes = lax.all_to_all(slopes, DP, 0, 0).astype(f32).sum(0)
    slopes = slopes + (sparsity_weight / TOK_DEV) * norms[None]
    dpre = jnp.where(pre > 0, slopes, 0.0)
    bias_rows = jnp.stack(pieces(dpre.sum(0))).reshape(3, 4, 384)
    loss_rows = jnp.broadcast_to(jnp.pad(jnp.stack(pieces(loss_z)), (0, 381)), (1, 4, 384))
    sent = jnp.concatenate(
        [dpre.astype(bf16).reshape(32, 4, 384), bias_rows, loss_rows, jnp.zeros((12, 4, 384), bf16)]
    )
    got = lax.all_to_all(sent.transpose(1, 0, 2), QUAD, 0, 0)
    bias_rows = jnp.stack(pieces(got[:, 32:35].astype(f32).sum((0, 1))))
    loss_row = jnp.pad(jnp.stack(pieces(got[:, 35, :3].astype(f32).sum())), (0, 381))[None]
    sent = jnp.concatenate(
        [got[:, :32].reshape(128, 384), bias_rows, loss_row, jnp.zeros((12, 384), bf16)]
    )
    got = share(sent, DP, 8)
    bias_grad = got[:, 128:131].astype(f32).sum((0, 1))
    loss = got[:, 131, :3].astype(f32).sum() / TOK_DEV
    dpre_every = got[:, :128].reshape(2, 4, 4, 32, 384).transpose(2, 0, 1, 3, 4)
    dpre_every = dpre_every.reshape(4, 2, 128, 384)

    x_every = lax.all_gather(x_quad, QUAD)
    gout_every = lax.all_gather(gout_quad, QUAD)
    acts_every = acts_quad.reshape(256, 4, 384).transpose(1, 0, 2)
    acts_every = lax.all_to_all(acts_every, QUAD, 0, 0).reshape(4, 2, 128, 384)
    enc_full = dot("qakt,qatj->kj", x_every, dpre_every)
    enc_full = enc_full.reshape(8, BLOCK, 384)[:, :108].reshape(8, 3, 36, 384)
    enc_grad = jnp.sum(jnp.where(pick[None, :, None, :], enc_full, 0.0), axis=1).reshape(288, 384)
    dec_full = dot("qakt,qatj->kj", gout_every, acts_every)
    dec_full = dec_full.reshape(8, BLOCK, 384)[:, :108].reshape(8, 3, 36, 384)
    dec_full = dec_full.transpose(1, 0, 2, 3).reshape(3, 288, 384)
    colsum = jnp.sum(acts_every.astype(f32), axis=(0, 1, 2))
    member = lax.axis_index(QUAD)
    own_norms = lax.dynamic_index_in_dim(norms.reshape(4, 384), member, 0, False)
    pull = (sparsity_weight / TOK_DEV) * colsum / own_norms
    dec_grad = jnp.where(reach[:, None, :], dec_full + pull * dec_t.astype(f32), 0.0)
    return (loss, recon, enc_grad.T, bias_grad, dec_grad.transpose(2, 0, 1))


def solution(mesh):
    fine = Mesh(np.asarray(mesh.devices).reshape(SIZES), ALL)
    in_specs = (
        P(DP, None, LATENT),
        P(DP, None, LATENT),
        P(LATENT, DP),
        P(LATENT),
        P(LATENT, None, DP),
        P(LATENT),
    )
    out_specs = (
        P(),
        P(DP, None, LATENT),
        P(LATENT, DP),
        P(LATENT),
        P(LATENT, None, DP),
    )
    return jax.shard_map(
        on_device, mesh=fine, in_specs=in_specs, out_specs=out_specs, check_vma=False
    )
```

```python
import jax
import jax.numpy as jnp
import numpy as np
from jax import lax
from jax.sharding import Mesh
from jax.sharding import PartitionSpec as P

LAYERS = 3
TOK_DEV = 128
SIZES = (4, 2, 16, 2, 2)
ALL = ("x", "yh", "z", "yl", "c")
DP = ("x", "yh")
LATENT = ("z", "yl", "c")
QUAD = ("yl", "c")
BLOCK = 112

sparsity_weight = 0.5
norm_epsilon = 1e-06
bf16, f32 = jnp.bfloat16, jnp.float32


def spread():
    pairs = []
    for a in range(8):
        for b in range(64):
            i, r = divmod(b, 8)
            pairs.append((a * 64 + b, i * 64 + ((a % 2) * 8 + r) * 4 + a // 2))
    return pairs


def pieces(value):
    high = lax.reduce_precision(value, 8, 7)
    middle = lax.reduce_precision(value - high, 8, 7)
    low = value - high - middle
    return [high.astype(bf16), middle.astype(bf16), low.astype(bf16)]


def share(block, axes, count):
    return lax.all_to_all(jnp.broadcast_to(block[None], (count, *block.shape)), axes, 0, 0)


def neighbour(block, axis):
    return lax.ppermute(block, axis, [(0, 1), (1, 0)])


def quad_of(block):
    pair = jnp.stack([block, neighbour(block, "yl")])
    other = neighbour(pair, "c")
    return jnp.stack([pair[0], other[0], pair[1], other[1]])


def relative(blocks):
    yl, c = lax.axis_index("yl"), lax.axis_index("c")
    blocks = jnp.where(yl == 1, blocks[jnp.array([2, 3, 0, 1])], blocks)
    return jnp.where(c == 1, blocks[jnp.array([1, 0, 3, 2])], blocks)


together = lax.optimization_barrier


def dot(spec, a, b):
    return jnp.einsum(spec, a, b, preferred_element_type=f32)


def on_device(resid, target, enc_weight, enc_bias, dec_weight, source):
    to = spread()
    back = [(d, s) for s, d in to]
    layer_ids = jnp.arange(LAYERS, dtype=jnp.int32)
    pick = source[None, :] == layer_ids[:, None]
    reach = source[None, :] <= layer_ids[:, None]

    both = jnp.stack([resid, target]).transpose(0, 2, 3, 1).reshape(2, 108, 128)
    both = jnp.pad(both, ((0, 0), (0, BLOCK - 108), (0, 0)))
    both, enc_weight, dec_weight = together((both, enc_weight, dec_weight))
    both = lax.ppermute(both, ALL, to)

    enc_t = enc_weight.T
    dec_t = jnp.where(reach[:, None, :], dec_weight.transpose(1, 2, 0), 0)
    square = jnp.sum(jnp.square(dec_t.astype(f32)), axis=(0, 1))
    extra = jnp.stack([source.astype(bf16), *pieces(enc_bias), *pieces(square)])
    enc_own = jnp.concatenate([enc_t, jnp.pad(extra, ((0, 9), (0, 0)))])
    enc_quad = quad_of(enc_own)
    dec_own = dec_t.reshape(3, 8, 36, 384).transpose(1, 0, 2, 3).reshape(8, 108, 384)
    dec_own = jnp.pad(dec_own, ((0, 0), (0, BLOCK - 108), (0, 0))).reshape(8 * BLOCK, 384)
    dec_own, both, enc_quad = together((dec_own, both, enc_quad))
    dec_quad = quad_of(dec_own)
    x_block, target_block = both[0], both[1]
    tail = enc_quad[:, 288:295].astype(f32)
    source_quad = tail[:, 0]
    bias_quad = (tail[:, 1] + tail[:, 2] + tail[:, 3]).reshape(1536)
    square_quad = (tail[:, 4] + tail[:, 5] + tail[:, 6]).reshape(1536)
    enc_rows = enc_quad[:, :288].reshape(4, 8, 1, 36, 384)
    pick_quad = source_quad[:, None, :] == layer_ids[None, :, None].astype(f32)
    enc_rows = jnp.where(pick_quad[:, None, :, None, :], enc_rows, 0).reshape(4, 8, 108, 384)
    enc_rows = jnp.pad(enc_rows, ((0, 0), (0, 0), (0, BLOCK - 108), (0, 0)))
    enc_rows = enc_rows.reshape(4, 8 * BLOCK, 384)

    x_quad = share(x_block, "z", 16).reshape(2, 8 * BLOCK, 128)
    x_quad, enc_rows, dec_quad = together((x_quad, enc_rows, dec_quad))
    partial = dot("akt,qkj->atqj", x_quad, enc_rows).reshape(8, 32, 1536)
    squares = jnp.broadcast_to(square_quad[None, None], (8, 8, 1536))
    summed = lax.all_to_all(jnp.concatenate([partial, squares], axis=1), DP, 0, 0).sum(0)
    pre = summed[:32] + bias_quad[None]
    norms = jnp.sqrt(summed[32] + norm_epsilon)
    acts = jnp.maximum(pre, 0.0).astype(bf16)
    sparsity = jnp.sum(acts.astype(f32) * norms[None], axis=0).reshape(12, 128).sum(0)
    acts_quad = share(acts, DP, 8).reshape(2, 128, 4, 384)

    terms = dot("qkj,atqj->akt", dec_quad, acts_quad).astype(bf16).reshape(16, BLOCK, 128)
    terms, acts_sent, x_sent = together((terms, acts_quad, x_quad))
    recon_sum = lax.all_to_all(terms, "z", 0, 0).astype(f32).sum(0)
    acts_sent = acts_sent.reshape(256, 4, 384).transpose(1, 0, 2)
    kept, away = acts_sent[:2], acts_sent[2:]
    away = neighbour(away, "yl")
    acts_every = jnp.stack([kept[0], away[0]])
    away = neighbour(jnp.stack([kept[1], away[1]]), "c")
    acts_every = jnp.stack([acts_every[0], away[0], acts_every[1], away[1]])
    acts_every = relative(acts_every).reshape(4, 2, 128, 384)
    recon_sum, acts_every = together((recon_sum, acts_every))
    x_every = lax.all_gather(x_sent, QUAD)
    error = recon_sum - target_block.astype(f32)
    local_loss = jnp.sum(error * error, axis=0) + sparsity_weight * sparsity
    gout = (2.0 * error / TOK_DEV).astype(bf16)
    row_ids = lax.broadcasted_iota(jnp.int32, (BLOCK, 128), 0)
    for row, piece in enumerate(pieces(local_loss)):
        gout = jnp.where(row_ids == 108 + row, piece[None], gout)
    gout, recon = together((gout, recon_sum.astype(bf16)))
    recon = lax.ppermute(recon, ALL, back)
    gout_all = share(gout, "z", 16)
    gout_all, recon = together((gout_all, recon))
    recon = recon[:108].reshape(3, 36, 128).transpose(2, 0, 1)
    loss_z = jnp.sum(gout_all[:, 108:111].astype(f32), axis=(0, 1))
    gout_quad = gout_all.reshape(2, 8 * BLOCK, 128)

    gout_every = lax.all_gather(gout_quad, QUAD)
    slopes = dot("akt,qkj->atqj", gout_quad, dec_quad).astype(bf16).reshape(8, 32, 1536)
    slopes = lax.all_to_all(slopes, DP, 0, 0).astype(f32).sum(0)
    slopes = slopes + (sparsity_weight / TOK_DEV) * norms[None]
    dpre = jnp.where(pre > 0, slopes, 0.0)
    bias_rows = jnp.stack(pieces(dpre.sum(0))).reshape(3, 4, 384)
    loss_rows = jnp.broadcast_to(jnp.concatenate(pieces(loss_z)), (1, 4, 384))
    sent = jnp.concatenate(
        [dpre.astype(bf16).reshape(32, 4, 384), bias_rows, loss_rows, jnp.zeros((12, 4, 384), bf16)]
    )
    got = lax.all_to_all(relative(sent.transpose(1, 0, 2)), QUAD, 0, 0)
    bias_rows = jnp.stack(pieces(got[:, 32:35].astype(f32).sum((0, 1))))
    loss_q = got[:, 35].astype(f32).sum(0).reshape(3, 128).sum(0)
    loss_row = jnp.concatenate(pieces(loss_q))[None]
    sent = jnp.concatenate(
        [got[:, :32].reshape(128, 384), bias_rows, loss_row, jnp.zeros((12, 384), bf16)]
    )
    got = share(sent, DP, 8)
    bias_grad = got[:, 128:131].astype(f32).sum((0, 1))
    loss = got[:, 131].astype(f32).sum() / TOK_DEV
    dpre_every = got[:, :128].reshape(2, 4, 4, 32, 384).transpose(2, 0, 1, 3, 4)
    dpre_every = dpre_every.reshape(4, 2, 128, 384)

    enc_full = dot("qakt,qatj->kj", x_every, dpre_every)
    enc_full = enc_full.reshape(8, BLOCK, 384)[:, :108].reshape(8, 3, 36, 384)
    enc_grad = jnp.sum(jnp.where(pick[None, :, None, :], enc_full, 0.0), axis=1).reshape(288, 384)
    dec_full = dot("qakt,qatj->kj", gout_every, acts_every)
    dec_full = dec_full.reshape(8, BLOCK, 384)[:, :108].reshape(8, 3, 36, 384)
    dec_full = dec_full.transpose(1, 0, 2, 3).reshape(3, 288, 384)
    colsum = jnp.sum(acts_every.astype(f32), axis=(0, 1, 2))
    own_norms = norms[:384]
    pull = (sparsity_weight / TOK_DEV) * colsum / own_norms
    dec_grad = jnp.where(reach[:, None, :], dec_full + pull * dec_t.astype(f32), 0.0)
    return (loss, recon, enc_grad.T, bias_grad, dec_grad.transpose(2, 0, 1))


def solution(mesh):
    fine = Mesh(np.asarray(mesh.devices).reshape(SIZES), ALL)
    in_specs = (
        P(DP, None, LATENT),
        P(DP, None, LATENT),
        P(LATENT, DP),
        P(LATENT),
        P(LATENT, None, DP),
        P(LATENT),
    )
    out_specs = (
        P(),
        P(DP, None, LATENT),
        P(LATENT, DP),
        P(LATENT),
        P(LATENT, None, DP),
    )
    return jax.shard_map(
        on_device, mesh=fine, in_specs=in_specs, out_specs=out_specs, check_vma=False
    )
```

```python
import jax
import jax.numpy as jnp
import numpy as np
from jax import lax
from jax.sharding import Mesh
from jax.sharding import PartitionSpec as P

LAYERS = 3
TOK_DEV = 128
SIZES = (4, 2, 16, 2, 2)
ALL = ("x", "yh", "z", "yl", "c")
DP = ("x", "yh")
LATENT = ("z", "yl", "c")
QUAD = ("yl", "c")
BLOCK = 112

sparsity_weight = 0.5
norm_epsilon = 1e-06
bf16, f32 = jnp.bfloat16, jnp.float32


def spread():
    pairs = []
    for a in range(8):
        for b in range(64):
            i, r = divmod(b, 8)
            pairs.append((a * 64 + b, i * 64 + ((a % 2) * 8 + r) * 4 + a // 2))
    return pairs


def pieces(value):
    high = lax.reduce_precision(value, 8, 7)
    middle = lax.reduce_precision(value - high, 8, 7)
    low = value - high - middle
    return [high.astype(bf16), middle.astype(bf16), low.astype(bf16)]


def share(block, axes, count):
    return lax.all_to_all(jnp.broadcast_to(block[None], (count, *block.shape)), axes, 0, 0)


def neighbour(block, axis):
    return lax.ppermute(block, axis, [(0, 1), (1, 0)])


def relative(blocks):
    yl, c = lax.axis_index("yl"), lax.axis_index("c")
    swapped = jnp.concatenate([blocks[2:], blocks[:2]])
    blocks = jnp.where(yl == 1, swapped, blocks)
    swapped = jnp.stack([blocks[1], blocks[0], blocks[3], blocks[2]])
    return jnp.where(c == 1, swapped, blocks)


together = lax.optimization_barrier


def dot(spec, a, b):
    return jnp.einsum(spec, a, b, preferred_element_type=f32)


def on_device(resid, target, enc_weight, enc_bias, dec_weight, source):
    to = spread()
    back = [(d, s) for s, d in to]
    layer_ids = jnp.arange(LAYERS, dtype=jnp.int32)
    pick = source[None, :] == layer_ids[:, None]
    reach = source[None, :] <= layer_ids[:, None]

    both = jnp.stack([resid, target]).transpose(0, 2, 3, 1).reshape(2, 108, 128)
    both = jnp.pad(both, ((0, 0), (0, BLOCK - 108), (0, 0)))
    both = lax.ppermute(both, ALL, to)
    x_block, target_block = both[0], both[1]

    enc_t = enc_weight.T
    dec_t = jnp.where(reach[:, None, :], dec_weight.transpose(1, 2, 0), 0)
    square = jnp.sum(jnp.square(dec_t.astype(f32)), axis=(0, 1))
    dec_own = dec_t.reshape(3, 8, 36, 384).transpose(1, 0, 2, 3).reshape(8, 108, 384)
    dec_own = jnp.pad(dec_own, ((0, 0), (0, BLOCK - 108), (0, 0))).reshape(8 * BLOCK, 384)
    extra = jnp.stack([source.astype(bf16), *pieces(enc_bias), *pieces(square)])
    enc_own = jnp.concatenate([enc_t, jnp.pad(extra, ((0, 9), (0, 0)))])
    enc_quad = lax.all_gather(enc_own, QUAD)
    dec_quad = lax.all_gather(dec_own, QUAD)
    tail = enc_quad[:, 288:295].astype(f32)
    source_quad = tail[:, 0]
    bias_quad = (tail[:, 1] + tail[:, 2] + tail[:, 3]).reshape(1536)
    square_quad = (tail[:, 4] + tail[:, 5] + tail[:, 6]).reshape(1536)
    enc_rows = enc_quad[:, :288].reshape(4, 8, 1, 36, 384)
    pick_quad = source_quad[:, None, :] == layer_ids[None, :, None].astype(f32)
    enc_rows = jnp.where(pick_quad[:, None, :, None, :], enc_rows, 0).reshape(4, 8, 108, 384)
    enc_rows = jnp.pad(enc_rows, ((0, 0), (0, 0), (0, BLOCK - 108), (0, 0)))
    enc_rows = enc_rows.reshape(4, 8 * BLOCK, 384)

    x_quad = share(x_block, "z", 16).reshape(2, 8 * BLOCK, 128)
    partial = dot("akt,qkj->atqj", x_quad, enc_rows).reshape(8, 32, 1536)
    squares = jnp.broadcast_to(square_quad[None, None], (8, 8, 1536))
    summed = lax.all_to_all(jnp.concatenate([partial, squares], axis=1), DP, 0, 0).sum(0)
    pre = summed[:32] + bias_quad[None]
    norms = jnp.sqrt(summed[32] + norm_epsilon)
    acts = jnp.maximum(pre, 0.0).astype(bf16)
    sparsity = jnp.sum(acts.astype(f32) * norms[None], axis=0).reshape(12, 128).sum(0)
    acts_quad = share(acts, DP, 8).reshape(2, 128, 4, 384)

    terms = dot("qkj,atqj->akt", dec_quad, acts_quad).astype(bf16).reshape(16, BLOCK, 128)
    terms, acts_sent = together((terms, acts_quad))
    recon_sum = lax.all_to_all(terms, "z", 0, 0).astype(f32).sum(0)
    acts_sent = relative(acts_sent.reshape(256, 4, 384).transpose(1, 0, 2))
    near, far = acts_sent[:2], neighbour(acts_sent[2:], "yl")
    mine = jnp.stack([near[0], far[0]])
    other = neighbour(jnp.stack([near[1], far[1]]), "c")
    acts_every = relative(jnp.stack([mine[0], other[0], mine[1], other[1]]))
    acts_every = acts_every.reshape(1024, 384)
    colsum = jnp.sum(acts_every.astype(f32), axis=0)
    recon_sum, acts_every, colsum = together((recon_sum, acts_every, colsum))
    acts_every = acts_every.reshape(4, 2, 128, 384)
    recon = lax.ppermute(recon_sum.astype(bf16), ALL, back)
    recon = recon[:108].reshape(3, 36, 128).transpose(2, 0, 1)
    error = recon_sum - target_block.astype(f32)
    local_loss = jnp.sum(error * error, axis=0) + sparsity_weight * sparsity
    gout = (2.0 * error / TOK_DEV).astype(bf16)
    row_ids = lax.broadcasted_iota(jnp.int32, (BLOCK, 128), 0)
    for row, piece in enumerate(pieces(local_loss)):
        gout = jnp.where(row_ids == 108 + row, piece[None], gout)
    gout_all = share(gout, "z", 16)
    loss_z = jnp.sum(gout_all[:, 108:111].astype(f32), axis=(0, 1))
    gout_quad = gout_all.reshape(2, 8 * BLOCK, 128)

    slopes = dot("akt,qkj->atqj", gout_quad, dec_quad).astype(bf16).reshape(8, 32, 1536)
    slopes = lax.all_to_all(slopes, DP, 0, 0).astype(f32).sum(0)
    slopes = slopes + (sparsity_weight / TOK_DEV) * norms[None]
    dpre = jnp.where(pre > 0, slopes, 0.0)
    bias_rows = jnp.stack(pieces(dpre.sum(0))).reshape(3, 4, 384)
    loss_rows = jnp.broadcast_to(jnp.concatenate(pieces(loss_z)), (1, 4, 384))
    sent = jnp.concatenate(
        [dpre.astype(bf16).reshape(32, 4, 384), bias_rows, loss_rows, jnp.zeros((12, 4, 384), bf16)]
    )
    got = lax.all_to_all(sent.transpose(1, 0, 2), QUAD, 0, 0)
    bias_rows = jnp.stack(pieces(got[:, 32:35].astype(f32).sum((0, 1))))
    loss_q = got[:, 35].astype(f32).sum(0).reshape(3, 128).sum(0)
    loss_row = jnp.concatenate(pieces(loss_q))[None]
    sent = jnp.concatenate(
        [got[:, :32].reshape(128, 384), bias_rows, loss_row, jnp.zeros((12, 384), bf16)]
    )
    got = share(sent, DP, 8)
    bias_grad = got[:, 128:131].astype(f32).sum((0, 1))
    loss = got[:, 131].astype(f32).sum() / TOK_DEV
    dpre_every = got[:, :128].reshape(2, 4, 4, 32, 384).transpose(2, 0, 1, 3, 4)
    dpre_every = dpre_every.reshape(4, 2, 128, 384)

    x_every = lax.all_gather(x_quad, QUAD)
    gout_every = lax.all_gather(gout_quad, QUAD)
    enc_full = dot("qakt,qatj->kj", x_every, dpre_every)
    enc_full = enc_full.reshape(8, BLOCK, 384)[:, :108].reshape(8, 3, 36, 384)
    enc_grad = jnp.sum(jnp.where(pick[None, :, None, :], enc_full, 0.0), axis=1).reshape(288, 384)
    dec_full = dot("qakt,qatj->kj", gout_every, acts_every)
    dec_full = dec_full.reshape(8, BLOCK, 384)[:, :108].reshape(8, 3, 36, 384)
    dec_full = dec_full.transpose(1, 0, 2, 3).reshape(3, 288, 384)
    member = lax.axis_index(QUAD)
    own_norms = lax.dynamic_index_in_dim(norms.reshape(4, 384), member, 0, False)
    pull = (sparsity_weight / TOK_DEV) * colsum / own_norms
    dec_grad = jnp.where(reach[:, None, :], dec_full + pull * dec_t.astype(f32), 0.0)
    return (loss, recon, enc_grad.T, bias_grad, dec_grad.transpose(2, 0, 1))


def solution(mesh):
    fine = Mesh(np.asarray(mesh.devices).reshape(SIZES), ALL)
    in_specs = (
        P(DP, None, LATENT),
        P(DP, None, LATENT),
        P(LATENT, DP),
        P(LATENT),
        P(LATENT, None, DP),
        P(LATENT),
    )
    out_specs = (
        P(),
        P(DP, None, LATENT),
        P(LATENT, DP),
        P(LATENT),
        P(LATENT, None, DP),
    )
    return jax.shard_map(
        on_device, mesh=fine, in_specs=in_specs, out_specs=out_specs, check_vma=False
    )
```

```python
import jax
import jax.numpy as jnp
import numpy as np
from jax import lax
from jax.experimental import pallas as pl
from jax.experimental.pallas import tpu as pltpu
from jax.sharding import Mesh
from jax.sharding import PartitionSpec as P

LAYERS = 3
TOK_DEV = 128
SIZES = (4, 2, 16, 2, 2)
ALL = ("x", "yh", "z", "yl", "c")
DP = ("x", "yh")
LATENT = ("z", "yl", "c")
QUAD = ("yl", "c")
BLOCK = 112

sparsity_weight = 0.5
norm_epsilon = 1e-06
bf16, f32 = jnp.bfloat16, jnp.float32


def spread():
    pairs = []
    for a in range(8):
        for b in range(64):
            i, r = divmod(b, 8)
            pairs.append((a * 64 + b, i * 64 + ((a % 2) * 8 + r) * 4 + a // 2))
    return pairs


def pieces(value):
    high = lax.reduce_precision(value, 8, 7)
    middle = lax.reduce_precision(value - high, 8, 7)
    low = value - high - middle
    return [high.astype(bf16), middle.astype(bf16), low.astype(bf16)]


def share(block, axes, count):
    return lax.all_to_all(jnp.broadcast_to(block[None], (count, *block.shape)), axes, 0, 0)


def call(kernel, *args, out):
    return pl.pallas_call(
        kernel,
        out_shape=[jax.ShapeDtypeStruct(shape, dtype) for shape, dtype in out],
        compiler_params=pltpu.CompilerParams(vmem_limit_bytes=40 * 1024 * 1024),
    )(*args)


def split(value):
    high = value.astype(bf16)
    rest = value - high.astype(f32)
    middle = rest.astype(bf16)
    return [high, middle, (rest - middle.astype(f32)).astype(bf16)]


def matmul(a, b, left, right):
    return lax.dot_general(a, b, (((left,), (right,)), ((), ())), preferred_element_type=f32)


def encode(x, rows, squares, out):
    for half in range(2):
        for q in range(4):
            product = matmul(x[half], rows[q], 0, 0)
            for g in range(4):
                for c in range(3):
                    at = (q * 3 + c) * 32
                    out[half * 4 + g, at : at + 32] = product[
                        g * 32 : g * 32 + 32, c * 128 : c * 128 + 128
                    ]
    for g in range(8):
        out[g, 384:] = squares[...]


def activate(parts, bias, pre, norms, acts, sparsity):
    total = jnp.sum(parts[...], axis=0)
    norm = jnp.sqrt(total[384:396] + norm_epsilon)
    norms[0:12] = norm
    norms[12:16] = jnp.zeros((4, 128), f32)
    weighted = jnp.zeros((32, 128), f32)
    for c in range(12):
        here = total[c * 32 : c * 32 + 32] + bias[c : c + 1]
        pre[c * 32 : c * 32 + 32] = here
        low = jnp.maximum(here, 0.0).astype(bf16)
        weighted = weighted + low.astype(f32) * norm[c : c + 1]
        for g in range(8):
            acts[g, c * 32 : c * 32 + 32] = low
    sparsity[...] = jnp.broadcast_to(jnp.sum(weighted, axis=0, keepdims=True), (8, 128))


def tokens_of(ref, half, column):
    return ref[half * 4 : half * 4 + 4, column * 32 : column * 32 + 32].reshape(128, 128)


def decode(rows, acts, out):
    for half in range(2):
        total = None
        for q in range(4):
            wide = jnp.concatenate([tokens_of(acts, half, q * 3 + c) for c in range(3)], axis=1)
            product = matmul(rows[q], wide, 1, 1)
            total = product if total is None else total + product
        low = total.astype(bf16)
        for r in range(8):
            out[half * 8 + r] = low[r * BLOCK : (r + 1) * BLOCK]


def compare(parts, target, sparsity, recon, gout):
    recon_sum = jnp.sum(parts[...].astype(f32), axis=0)
    recon[...] = recon_sum.astype(bf16)
    error = recon_sum - target[...].astype(f32)
    by_lane = jnp.sum(error * error, axis=0, keepdims=True) + sparsity_weight * sparsity[0:1]
    slope = 2.0 * error / TOK_DEV
    row = lax.broadcasted_iota(jnp.int32, (BLOCK, 128), 0)
    for k, piece in enumerate(split(by_lane)):
        slope = jnp.where(row == 108 + k, piece.astype(f32), slope)
    low = slope.astype(bf16)
    for z in range(16):
        gout[z] = low


def pull_back(gout, rows, out, loss):
    total = jnp.sum(gout[:, 96:112].astype(f32), axis=0)
    loss[...] = jnp.broadcast_to(jnp.sum(total[12:15], axis=0, keepdims=True), (8, 128))
    for half in range(2):
        tokens = jnp.concatenate([gout[half * 8 + r] for r in range(8)], axis=0)
        for q in range(4):
            product = matmul(tokens, rows[q], 0, 0).astype(bf16)
            for g in range(4):
                for c in range(3):
                    at = (q * 3 + c) * 32
                    out[half * 4 + g, at : at + 32] = product[
                        g * 32 : g * 32 + 32, c * 128 : c * 128 + 128
                    ]


def tail_of(values):
    row = lax.broadcasted_iota(jnp.int32, (16, 128), 0)
    tail = jnp.zeros((16, 128), f32)
    for k, value in enumerate(values):
        for p, piece in enumerate(split(value)):
            tail = jnp.where(row == 4 * p + k, piece.astype(f32), tail)
    return tail.astype(bf16)


def slopes_of(parts, pre, norms, loss, out):
    total = jnp.sum(parts[...].astype(f32), axis=0)
    for q in range(4):
        sums = []
        for c in range(3):
            k = q * 3 + c
            slope = total[k * 32 : k * 32 + 32] + (sparsity_weight / TOK_DEV) * norms[k : k + 1]
            slope = jnp.where(pre[k * 32 : k * 32 + 32] > 0, slope, 0.0)
            sums.append(jnp.sum(slope, axis=0, keepdims=True))
            out[q, c * 32 : c * 32 + 32] = slope.astype(bf16)
        out[q, 96:112] = tail_of([*sums, loss[0:1]])


def regroup(got, out):
    tail = jnp.sum(got[:, 96:112].astype(f32), axis=0)
    tail = tail[0:4] + tail[4:8] + tail[8:12]
    tail = tail_of([tail[k : k + 1] for k in range(4)])
    for g in range(8):
        for q in range(4):
            out[g, q * 96 : q * 96 + 96] = got[q, 0:96]
        out[g, 384:400] = tail


def over_tokens(blocks, values, out):
    total = None
    for q in range(4):
        wide = jnp.concatenate([blocks[q, 0], blocks[q, 1]], axis=1)
        column = lambda c: jnp.concatenate([tokens_of(values, h, q * 3 + c) for h in range(2)], axis=0)
        product = matmul(wide, jnp.concatenate([column(c) for c in range(3)], axis=1), 1, 0)
        total = product if total is None else total + product
    out[...] = total


def neighbour(block, axis):
    return lax.ppermute(block, axis, [(0, 1), (1, 0)])


def relative(blocks):
    yl, c = lax.axis_index("yl"), lax.axis_index("c")
    swapped = jnp.concatenate([blocks[2:], blocks[:2]])
    blocks = jnp.where(yl == 1, swapped, blocks)
    swapped = jnp.stack([blocks[1], blocks[0], blocks[3], blocks[2]])
    return jnp.where(c == 1, swapped, blocks)


together = lax.optimization_barrier


def on_device(resid, target, enc_weight, enc_bias, dec_weight, source):
    to = spread()
    back = [(d, s) for s, d in to]
    layer_ids = jnp.arange(LAYERS, dtype=jnp.int32)
    pick = source[None, :] == layer_ids[:, None]
    reach = source[None, :] <= layer_ids[:, None]

    both = jnp.stack([resid, target]).transpose(0, 2, 3, 1).reshape(2, 108, 128)
    both = jnp.pad(both, ((0, 0), (0, BLOCK - 108), (0, 0)))
    both = lax.ppermute(both, ALL, to)
    x_block, target_block = both[0], both[1]

    enc_t = enc_weight.T
    dec_t = jnp.where(reach[:, None, :], dec_weight.transpose(1, 2, 0), 0)
    square = jnp.sum(jnp.square(dec_t.astype(f32)), axis=(0, 1))
    dec_own = dec_t.reshape(3, 8, 36, 384).transpose(1, 0, 2, 3).reshape(8, 108, 384)
    dec_own = jnp.pad(dec_own, ((0, 0), (0, BLOCK - 108), (0, 0))).reshape(8 * BLOCK, 384)
    extra = jnp.stack([source.astype(bf16), *pieces(enc_bias), *pieces(square)])
    enc_own = jnp.concatenate([enc_t, jnp.pad(extra, ((0, 9), (0, 0)))])
    enc_quad = lax.all_gather(enc_own, QUAD)
    dec_quad = lax.all_gather(dec_own, QUAD)
    tail = enc_quad[:, 288:295].astype(f32)
    source_quad = tail[:, 0]
    bias_quad = (tail[:, 1] + tail[:, 2] + tail[:, 3]).reshape(1536)
    square_quad = (tail[:, 4] + tail[:, 5] + tail[:, 6]).reshape(1536)
    enc_rows = enc_quad[:, :288].reshape(4, 8, 1, 36, 384)
    pick_quad = source_quad[:, None, :] == layer_ids[None, :, None].astype(f32)
    enc_rows = jnp.where(pick_quad[:, None, :, None, :], enc_rows, 0).reshape(4, 8, 108, 384)
    enc_rows = jnp.pad(enc_rows, ((0, 0), (0, 0), (0, BLOCK - 108), (0, 0)))
    enc_rows = enc_rows.reshape(4, 8 * BLOCK, 384)

    x_quad = share(x_block, "z", 16).reshape(2, 8 * BLOCK, 128)
    squares = jnp.pad(square_quad.reshape(12, 128), ((0, 4), (0, 0)))
    (partial,) = call(encode, x_quad, enc_rows, squares, out=[((8, 400, 128), f32)])
    partial = lax.all_to_all(partial, DP, 0, 0)
    pre, norms, acts, sparsity = call(
        activate,
        partial,
        bias_quad.reshape(12, 128),
        out=[((384, 128), f32), ((16, 128), f32), ((8, 384, 128), bf16), ((8, 128), f32)],
    )
    acts_quad = lax.all_to_all(acts, DP, 0, 0)

    (terms,) = call(decode, dec_quad, acts_quad, out=[((16, BLOCK, 128), bf16)])
    terms, acts_sent = together((terms, acts_quad))
    parts = lax.all_to_all(terms, "z", 0, 0)
    acts_sent = relative(acts_sent.reshape(8, 4, 96, 128).transpose(1, 0, 2, 3))
    near, far = acts_sent[:2], neighbour(acts_sent[2:], "yl")
    mine = jnp.stack([near[0], far[0]])
    other = neighbour(jnp.stack([near[1], far[1]]), "c")
    acts_every = relative(jnp.stack([mine[0], other[0], mine[1], other[1]]))
    acts_every = acts_every.transpose(1, 0, 2, 3).reshape(8, 384, 128)
    colsum = jnp.sum(acts_every.reshape(8, 4, 3, 32, 128).astype(f32), axis=(0, 1, 3)).reshape(384)
    parts, acts_every, colsum = together((parts, acts_every, colsum))
    recon, gout = call(
        compare,
        parts,
        target_block,
        sparsity,
        out=[((BLOCK, 128), bf16), ((16, BLOCK, 128), bf16)],
    )
    gout_all = lax.all_to_all(gout, "z", 0, 0)

    gout_every = lax.all_gather(gout_all.reshape(2, 8 * BLOCK, 128), QUAD)
    slopes, loss_z = call(
        pull_back, gout_all, dec_quad, out=[((8, 384, 128), bf16), ((8, 128), f32)]
    )
    slopes = lax.all_to_all(slopes, DP, 0, 0)
    (sent,) = call(slopes_of, slopes, pre, norms, loss_z, out=[((4, 112, 128), bf16)])
    got = lax.all_to_all(sent, QUAD, 0, 0)
    (sent,) = call(regroup, got, out=[((8, 400, 128), bf16)])
    got = lax.all_to_all(sent, DP, 0, 0)

    (dec_full,) = call(over_tokens, gout_every, acts_every, out=[((8 * BLOCK, 384), f32)])
    dec_full = dec_full.reshape(8, BLOCK, 384)[:, :108].reshape(8, 3, 36, 384)
    dec_full = dec_full.transpose(1, 0, 2, 3).reshape(3, 288, 384)
    member = lax.axis_index(QUAD)
    own_norms = lax.dynamic_index_in_dim(norms[:12].reshape(4, 384), member, 0, False)
    pull = (sparsity_weight / TOK_DEV) * colsum / own_norms
    dec_grad = jnp.where(reach[:, None, :], dec_full + pull * dec_t.astype(f32), 0.0)
    got, dec_grad = together((got, dec_grad))
    x_every = lax.all_gather(x_quad, QUAD)
    (enc_full,) = call(over_tokens, x_every, got, out=[((8 * BLOCK, 384), f32)])
    enc_full = enc_full.reshape(8, BLOCK, 384)[:, :108].reshape(8, 3, 36, 384)
    enc_grad = jnp.sum(jnp.where(pick[None, :, None, :], enc_full, 0.0), axis=1).reshape(288, 384)
    tail = got[:, 384:396].astype(f32).sum(0).reshape(3, 4, 128).sum(0)
    bias_grad = tail[:3].reshape(384)
    loss = tail[3].sum() / TOK_DEV
    recon = lax.ppermute(recon, ALL, back)
    recon, enc_grad = together((recon, enc_grad))
    recon = recon[:108].reshape(3, 36, 128).transpose(2, 0, 1)
    return (loss, recon, enc_grad.T, bias_grad, dec_grad.transpose(2, 0, 1))


def solution(mesh):
    fine = Mesh(np.asarray(mesh.devices).reshape(SIZES), ALL)
    in_specs = (
        P(DP, None, LATENT),
        P(DP, None, LATENT),
        P(LATENT, DP),
        P(LATENT),
        P(LATENT, None, DP),
        P(LATENT),
    )
    out_specs = (
        P(),
        P(DP, None, LATENT),
        P(LATENT, DP),
        P(LATENT),
        P(LATENT, None, DP),
    )
    return jax.shard_map(
        on_device, mesh=fine, in_specs=in_specs, out_specs=out_specs, check_vma=False
    )
```

```python
import jax
import jax.numpy as jnp
import numpy as np
from jax import lax
from jax.experimental import pallas as pl
from jax.experimental.pallas import tpu as pltpu
from jax.sharding import Mesh
from jax.sharding import PartitionSpec as P

LAYERS = 3
TOK_DEV = 128
SIZES = (4, 2, 16, 2, 2)
ALL = ("x", "yh", "z", "yl", "c")
DP = ("x", "yh")
LATENT = ("z", "yl", "c")
QUAD = ("yl", "c")
PLANE = ("yh", "yl", "c")
BLOCK = 112

sparsity_weight = 0.5
norm_epsilon = 1e-06
bf16, f32 = jnp.bfloat16, jnp.float32


def spread():
    pairs = []
    for a in range(8):
        for b in range(64):
            i, r = divmod(b, 8)
            pairs.append((a * 64 + b, i * 64 + ((a % 2) * 8 + r) * 4 + a // 2))
    return pairs


def pieces(value):
    high = lax.reduce_precision(value, 8, 7)
    middle = lax.reduce_precision(value - high, 8, 7)
    low = value - high - middle
    return [high.astype(bf16), middle.astype(bf16), low.astype(bf16)]


def share(block, axes, count):
    return lax.all_to_all(jnp.broadcast_to(block[None], (count, *block.shape)), axes, 0, 0)


def call(kernel, *args, out, scratch=()):
    return pl.pallas_call(
        kernel,
        out_shape=[jax.ShapeDtypeStruct(shape, dtype) for shape, dtype in out],
        scratch_shapes=scratch,
        compiler_params=pltpu.CompilerParams(vmem_limit_bytes=40 * 1024 * 1024),
    )(*args)


def split(value):
    high = value.astype(bf16)
    rest = value - high.astype(f32)
    middle = rest.astype(bf16)
    return [high, middle, (rest - middle.astype(f32)).astype(bf16)]


def matmul(a, b, left, right):
    return lax.dot_general(a, b, (((left,), (right,)), ((), ())), preferred_element_type=f32)


def encode(x, rows, squares, out):
    for half in range(2):
        for q in range(4):
            product = matmul(x[half], rows[q], 0, 0)
            for g in range(4):
                for c in range(3):
                    at = (q * 3 + c) * 32
                    out[half * 4 + g, at : at + 32] = product[
                        g * 32 : g * 32 + 32, c * 128 : c * 128 + 128
                    ]
    for g in range(8):
        out[g, 384:] = squares[...]


def activate(parts, bias, pre, norms, acts, sparsity):
    total = jnp.sum(parts[...], axis=0)
    norm = jnp.sqrt(total[384:396] + norm_epsilon)
    norms[0:12] = norm
    norms[12:16] = jnp.zeros((4, 128), f32)
    weighted = jnp.zeros((32, 128), f32)
    for c in range(12):
        here = total[c * 32 : c * 32 + 32] + bias[c : c + 1]
        pre[c * 32 : c * 32 + 32] = here
        low = jnp.maximum(here, 0.0).astype(bf16)
        weighted = weighted + low.astype(f32) * norm[c : c + 1]
        for g in range(8):
            acts[g, c * 32 : c * 32 + 32] = low
    sparsity[...] = jnp.broadcast_to(jnp.sum(weighted, axis=0, keepdims=True), (8, 128))


def tokens_of(ref, half, column):
    return ref[half * 4 : half * 4 + 4, column * 32 : column * 32 + 32].reshape(128, 128)


def decode(rows, acts, out):
    for half in range(2):
        total = None
        for q in range(4):
            wide = jnp.concatenate([tokens_of(acts, half, q * 3 + c) for c in range(3)], axis=1)
            product = matmul(rows[q], wide, 1, 1)
            total = product if total is None else total + product
        low = total.astype(bf16)
        for r in range(8):
            out[half * 8 + r] = low[r * BLOCK : (r + 1) * BLOCK]


def compare(parts, target, sparsity, recon, gout):
    recon_sum = jnp.sum(parts[...].astype(f32), axis=0)
    recon[...] = recon_sum.astype(bf16)
    error = recon_sum - target[...].astype(f32)
    by_lane = jnp.sum(error * error, axis=0, keepdims=True) + sparsity_weight * sparsity[0:1]
    slope = 2.0 * error / TOK_DEV
    row = lax.broadcasted_iota(jnp.int32, (BLOCK, 128), 0)
    for k, piece in enumerate(split(by_lane)):
        slope = jnp.where(row == 108 + k, piece.astype(f32), slope)
    low = slope.astype(bf16)
    for z in range(16):
        gout[z] = low


def pull_back(gout, rows, out, loss):
    total = jnp.sum(gout[:, 96:112].astype(f32), axis=0)
    loss[...] = jnp.broadcast_to(jnp.sum(total[12:15], axis=0, keepdims=True), (8, 128))
    for half in range(2):
        tokens = jnp.concatenate([gout[half * 8 + r] for r in range(8)], axis=0)
        for q in range(4):
            product = matmul(tokens, rows[q], 0, 0).astype(bf16)
            for g in range(4):
                for c in range(3):
                    at = (q * 3 + c) * 32
                    out[half * 4 + g, at : at + 32] = product[
                        g * 32 : g * 32 + 32, c * 128 : c * 128 + 128
                    ]


def tail_of(values):
    row = lax.broadcasted_iota(jnp.int32, (16, 128), 0)
    tail = jnp.zeros((16, 128), f32)
    for k, value in enumerate(values):
        for p, piece in enumerate(split(value)):
            tail = jnp.where(row == 4 * p + k, piece.astype(f32), tail)
    return tail.astype(bf16)


def slopes_of(parts, pre, norms, loss, out):
    total = jnp.sum(parts[...].astype(f32), axis=0)
    for q in range(4):
        sums = []
        for c in range(3):
            k = q * 3 + c
            slope = total[k * 32 : k * 32 + 32] + (sparsity_weight / TOK_DEV) * norms[k : k + 1]
            slope = jnp.where(pre[k * 32 : k * 32 + 32] > 0, slope, 0.0)
            sums.append(jnp.sum(slope, axis=0, keepdims=True))
            for yh in range(2):
                out[yh * 4 + q, c * 32 : c * 32 + 32] = slope.astype(bf16)
        tail = tail_of([*sums, loss[0:1]])
        for yh in range(2):
            out[yh * 4 + q, 96:112] = tail


def regroup(got, out):
    tail = jnp.sum(got[:, 96:112].astype(f32), axis=0)
    tail = tail[0:4] + tail[4:8] + tail[8:12]
    tail = tail_of([tail[k : k + 1] for k in range(4)])
    for x in range(4):
        for m in range(8):
            out[x, m * 96 : m * 96 + 96] = got[m, 0:96]
        out[x, 768:784] = tail


def over_tokens(blocks, values):
    total = None
    for q in range(4):
        wide = jnp.concatenate([blocks[q, 0], blocks[q, 1]], axis=1)
        column = lambda c: jnp.concatenate([values(h, q, c) for h in range(2)], axis=0)
        product = matmul(wide, jnp.concatenate([column(c) for c in range(3)], axis=1), 1, 0)
        total = product if total is None else total + product
    return total


def decoder_gradient(blocks, acts, rows, pull, reach, out, total):
    total[...] = over_tokens(blocks, lambda h, q, c: tokens_of(acts, h, q * 3 + c))
    for layer in range(LAYERS):
        for r in range(8):
            at = r * BLOCK + layer * 36
            out[layer, r * 36 : r * 36 + 36] = total[at : at + 36]
        whole = out[layer] + pull[0:1] * rows[layer].astype(f32)
        out[layer] = jnp.where(reach[layer : layer + 1] > 0, whole, 0.0)


def encoder_gradient(blocks, dpre, pick, out, sums, total):
    def values(half, q, c):
        parts = [
            dpre[half * 2 + g // 2, pl.ds(((g % 2) * 4 + q) * 96 + c * 32, 32)] for g in range(4)
        ]
        return jnp.concatenate(parts, axis=0)

    total[...] = over_tokens(blocks, values)
    for r in range(8):
        own = jnp.zeros((36, 384), f32)
        for layer in range(LAYERS):
            at = r * BLOCK + layer * 36
            own = own + jnp.where(pick[layer : layer + 1] > 0, total[at : at + 36], 0.0)
        out[r * 36 : r * 36 + 36] = own
    tail = jnp.sum(dpre[:, 768:784].astype(f32), axis=0)
    sums[0:4] = tail[0:4] + tail[4:8] + tail[8:12]
    sums[4:8] = jnp.zeros((4, 128), f32)


def neighbour(block, axis):
    return lax.ppermute(block, axis, [(0, 1), (1, 0)])


def relative(blocks):
    yl, c = lax.axis_index("yl"), lax.axis_index("c")
    swapped = jnp.concatenate([blocks[2:], blocks[:2]])
    blocks = jnp.where(yl == 1, swapped, blocks)
    swapped = jnp.stack([blocks[1], blocks[0], blocks[3], blocks[2]])
    return jnp.where(c == 1, swapped, blocks)


together = lax.optimization_barrier


def on_device(resid, target, enc_weight, enc_bias, dec_weight, source):
    to = spread()
    back = [(d, s) for s, d in to]
    layer_ids = jnp.arange(LAYERS, dtype=jnp.int32)
    pick = source[None, :] == layer_ids[:, None]
    reach = source[None, :] <= layer_ids[:, None]

    both = jnp.stack([resid, target]).transpose(0, 2, 3, 1).reshape(2, 108, 128)
    both = jnp.pad(both, ((0, 0), (0, BLOCK - 108), (0, 0)))
    both = lax.ppermute(both, ALL, to)
    x_block, target_block = both[0], both[1]

    enc_t = enc_weight.T
    dec_t = jnp.where(reach[:, None, :], dec_weight.transpose(1, 2, 0), 0)
    square = jnp.sum(jnp.square(dec_t.astype(f32)), axis=(0, 1))
    dec_own = dec_t.reshape(3, 8, 36, 384).transpose(1, 0, 2, 3).reshape(8, 108, 384)
    dec_own = jnp.pad(dec_own, ((0, 0), (0, BLOCK - 108), (0, 0))).reshape(8 * BLOCK, 384)
    extra = jnp.stack([source.astype(bf16), *pieces(enc_bias), *pieces(square)])
    enc_own = jnp.concatenate([enc_t, jnp.pad(extra, ((0, 9), (0, 0)))])
    enc_quad = lax.all_gather(enc_own, QUAD)
    dec_quad = lax.all_gather(dec_own, QUAD)
    tail = enc_quad[:, 288:295].astype(f32)
    source_quad = tail[:, 0]
    bias_quad = (tail[:, 1] + tail[:, 2] + tail[:, 3]).reshape(1536)
    square_quad = (tail[:, 4] + tail[:, 5] + tail[:, 6]).reshape(1536)
    enc_rows = enc_quad[:, :288].reshape(4, 8, 1, 36, 384)
    pick_quad = source_quad[:, None, :] == layer_ids[None, :, None].astype(f32)
    enc_rows = jnp.where(pick_quad[:, None, :, None, :], enc_rows, 0).reshape(4, 8, 108, 384)
    enc_rows = jnp.pad(enc_rows, ((0, 0), (0, 0), (0, BLOCK - 108), (0, 0)))
    enc_rows = enc_rows.reshape(4, 8 * BLOCK, 384)

    x_quad = share(x_block, "z", 16).reshape(2, 8 * BLOCK, 128)
    squares = jnp.pad(square_quad.reshape(12, 128), ((0, 4), (0, 0)))
    x_quad, dec_quad = together((x_quad, dec_quad))
    (partial,) = call(encode, x_quad, enc_rows, squares, out=[((8, 400, 128), f32)])
    partial = lax.all_to_all(partial, DP, 0, 0)
    pre, norms, acts, sparsity = call(
        activate,
        partial,
        bias_quad.reshape(12, 128),
        out=[((384, 128), f32), ((16, 128), f32), ((8, 384, 128), bf16), ((8, 128), f32)],
    )
    acts_quad = lax.all_to_all(acts, DP, 0, 0)

    (terms,) = call(decode, dec_quad, acts_quad, out=[((16, BLOCK, 128), bf16)])
    terms, acts_sent = together((terms, acts_quad))
    parts = lax.all_to_all(terms, "z", 0, 0)
    acts_sent = relative(acts_sent.reshape(8, 4, 96, 128).transpose(1, 0, 2, 3))
    near, far = acts_sent[:2], neighbour(acts_sent[2:], "yl")
    mine = jnp.stack([near[0], far[0]])
    other = neighbour(jnp.stack([near[1], far[1]]), "c")
    acts_every = relative(jnp.stack([mine[0], other[0], mine[1], other[1]]))
    acts_every = acts_every.transpose(1, 0, 2, 3).reshape(8, 384, 128)
    colsum = jnp.sum(acts_every.reshape(8, 4, 3, 32, 128).astype(f32), axis=(0, 1, 3)).reshape(384)
    parts, acts_every, colsum = together((parts, acts_every, colsum))
    recon, gout = call(
        compare,
        parts,
        target_block,
        sparsity,
        out=[((BLOCK, 128), bf16), ((16, BLOCK, 128), bf16)],
    )
    x_every = lax.all_gather(x_quad, QUAD)
    gout, x_every = together((gout, x_every))
    gout_all = lax.all_to_all(gout, "z", 0, 0)

    gout_every = lax.all_gather(gout_all.reshape(2, 8 * BLOCK, 128), QUAD)
    slopes, loss_z = call(
        pull_back, gout_all, dec_quad, out=[((8, 384, 128), bf16), ((8, 128), f32)]
    )
    slopes = lax.all_to_all(slopes, DP, 0, 0)
    (sent,) = call(slopes_of, slopes, pre, norms, loss_z, out=[((8, 112, 128), bf16)])
    got = lax.all_to_all(sent, PLANE, 0, 0)
    (sent,) = call(regroup, got, out=[((4, 784, 128), bf16)])
    got = lax.all_to_all(sent, "x", 0, 0)

    total = pltpu.VMEM((8 * BLOCK, 384), f32)
    member = lax.axis_index(QUAD)
    own_norms = lax.dynamic_index_in_dim(norms[:12].reshape(4, 384), member, 0, False)
    pull = ((sparsity_weight / TOK_DEV) * colsum / own_norms)[None]
    (dec_grad,) = call(
        decoder_gradient,
        gout_every,
        acts_every,
        dec_t,
        pull,
        reach.astype(f32),
        out=[((LAYERS, 288, 384), f32)],
        scratch=[total],
    )
    got, dec_grad = together((got, dec_grad))
    enc_grad, sums = call(
        encoder_gradient,
        x_every,
        got,
        pick.astype(f32),
        out=[((288, 384), f32), ((8, 128), f32)],
        scratch=[total],
    )
    bias_grad = sums[:3].reshape(384)
    loss = sums[3].sum() / TOK_DEV
    recon = lax.ppermute(recon, ALL, back)
    recon, enc_grad = together((recon, enc_grad))
    recon = recon[:108].reshape(3, 36, 128).transpose(2, 0, 1)
    return (loss, recon, enc_grad.T, bias_grad, dec_grad.transpose(2, 0, 1))


def solution(mesh):
    fine = Mesh(np.asarray(mesh.devices).reshape(SIZES), ALL)
    in_specs = (
        P(DP, None, LATENT),
        P(DP, None, LATENT),
        P(LATENT, DP),
        P(LATENT),
        P(LATENT, None, DP),
        P(LATENT),
    )
    out_specs = (
        P(),
        P(DP, None, LATENT),
        P(LATENT, DP),
        P(LATENT),
        P(LATENT, None, DP),
    )
    return jax.shard_map(
        on_device, mesh=fine, in_specs=in_specs, out_specs=out_specs, check_vma=False
    )
```

```python
import jax
import jax.numpy as jnp
import numpy as np
from jax import lax
from jax.experimental import pallas as pl
from jax.experimental.pallas import tpu as pltpu
from jax.sharding import Mesh
from jax.sharding import PartitionSpec as P

LAYERS = 3
TOK_DEV = 128
SIZES = (4, 2, 16, 2, 2)
ALL = ("x", "yh", "z", "yl", "c")
DP = ("x", "yh")
LATENT = ("z", "yl", "c")
QUAD = ("yl", "c")
PLANE = ("yh", "yl", "c")
BLOCK = 112

sparsity_weight = 0.5
norm_epsilon = 1e-06
bf16, f32 = jnp.bfloat16, jnp.float32


PAIRS = ((0, 5), (1, 4), (2, 7), (3, 6))


def ring(a, b, size):
    return min((a - b) % size, (b - a) % size)


def placing(i, q):
    x, yh = divmod(i, 2)
    hops = []
    for a in PAIRS[q]:
        for r in range(8):
            beside = ring(a // 2, x, 4) + ring(2 * (a % 2) + r % 4 // 2, 2 * yh + q // 2, 4)
            hops.append([beside + ring(2 * i + r // 4, z, 16) for z in range(16)])

    def seat(block, seen):
        for z in range(16):
            if hops[block][z] <= most and z not in seen:
                seen.add(z)
                if owner[z] is None or seat(owner[z], seen):
                    owner[z] = block
                    return True
        return False

    for most in range(16):
        owner = [None] * 16
        if all(seat(block, set()) for block in range(16)):
            return [owner.index(block) for block in range(16)]


PLACE = [[placing(i, q) for q in range(4)] for i in range(8)]


def spread():
    pairs = []
    for i in range(8):
        for q in range(4):
            for block, z in enumerate(PLACE[i][q]):
                half, r = divmod(block, 8)
                pairs.append((PAIRS[q][half] * 64 + 8 * i + r, i * 64 + z * 4 + q))
    return pairs


def pieces(value):
    high = lax.reduce_precision(value, 8, 7)
    middle = lax.reduce_precision(value - high, 8, 7)
    low = value - high - middle
    return [high.astype(bf16), middle.astype(bf16), low.astype(bf16)]


def share(block, axes, count):
    return lax.all_to_all(jnp.broadcast_to(block[None], (count, *block.shape)), axes, 0, 0)


def call(kernel, *args, out, scratch=()):
    def place(arg):
        if arg.dtype == jnp.int32:
            return pl.BlockSpec(memory_space=pltpu.SMEM)
        if arg.shape == (4, 16, BLOCK, 128):
            return pl.BlockSpec(memory_space=pl.ANY)
        return pl.BlockSpec(memory_space=pltpu.VMEM)

    return pl.pallas_call(
        kernel,
        in_specs=[place(arg) for arg in args],
        out_shape=[jax.ShapeDtypeStruct(shape, dtype) for shape, dtype in out],
        scratch_shapes=scratch,
        compiler_params=pltpu.CompilerParams(vmem_limit_bytes=(58 if scratch else 40) * 2**20),
    )(*args)


def split(value):
    high = value.astype(bf16)
    rest = value - high.astype(f32)
    middle = rest.astype(bf16)
    return [high, middle, (rest - middle.astype(f32)).astype(bf16)]


def matmul(a, b, left, right):
    return lax.dot_general(a, b, (((left,), (right,)), ((), ())), preferred_element_type=f32)


def encode(at_z, x, rows, squares, out):
    for half in range(2):
        tokens = jnp.concatenate([x[at_z[half * 8 + r]] for r in range(8)], axis=0)
        for q in range(4):
            product = matmul(tokens, rows[q], 0, 0)
            for g in range(4):
                for c in range(3):
                    at = (q * 3 + c) * 32
                    out[half * 4 + g, at : at + 32] = product[
                        g * 32 : g * 32 + 32, c * 128 : c * 128 + 128
                    ]
    for g in range(8):
        out[g, 384:] = squares[...]


def activate(parts, bias, pre, norms, acts, sparsity):
    total = jnp.sum(parts[...], axis=0)
    norm = jnp.sqrt(total[384:396] + norm_epsilon)
    norms[0:12] = norm
    norms[12:16] = jnp.zeros((4, 128), f32)
    weighted = jnp.zeros((32, 128), f32)
    for c in range(12):
        here = total[c * 32 : c * 32 + 32] + bias[c : c + 1]
        pre[c * 32 : c * 32 + 32] = here
        low = jnp.maximum(here, 0.0).astype(bf16)
        weighted = weighted + low.astype(f32) * norm[c : c + 1]
        for g in range(8):
            acts[g, c * 32 : c * 32 + 32] = low
    sparsity[...] = jnp.broadcast_to(jnp.sum(weighted, axis=0, keepdims=True), (8, 128))


def tokens_of(ref, half, column):
    return ref[half * 4 : half * 4 + 4, column * 32 : column * 32 + 32].reshape(128, 128)


def decode(at_z, rows, acts, out):
    for half in range(2):
        total = None
        for q in range(4):
            wide = jnp.concatenate([tokens_of(acts, half, q * 3 + c) for c in range(3)], axis=1)
            product = matmul(rows[q], wide, 1, 1)
            total = product if total is None else total + product
        low = total.astype(bf16)
        for r in range(8):
            out[at_z[half * 8 + r]] = low[r * BLOCK : (r + 1) * BLOCK]


def compare(parts, target, sparsity, recon, gout):
    recon_sum = jnp.sum(parts[...].astype(f32), axis=0)
    recon[...] = recon_sum.astype(bf16)
    error = recon_sum - target[...].astype(f32)
    by_lane = jnp.sum(error * error, axis=0, keepdims=True) + sparsity_weight * sparsity[0:1]
    slope = 2.0 * error / TOK_DEV
    row = lax.broadcasted_iota(jnp.int32, (BLOCK, 128), 0)
    for k, piece in enumerate(split(by_lane)):
        slope = jnp.where(row == 108 + k, piece.astype(f32), slope)
    low = slope.astype(bf16)
    for z in range(16):
        gout[z] = low


def pull_back(at_z, gout, rows, out, loss):
    total = jnp.sum(gout[:, 96:112].astype(f32), axis=0)
    loss[...] = jnp.broadcast_to(jnp.sum(total[12:15], axis=0, keepdims=True), (8, 128))
    for half in range(2):
        tokens = jnp.concatenate([gout[at_z[half * 8 + r]] for r in range(8)], axis=0)
        for q in range(4):
            product = matmul(tokens, rows[q], 0, 0).astype(bf16)
            for g in range(4):
                for c in range(3):
                    at = (q * 3 + c) * 32
                    out[half * 4 + g, at : at + 32] = product[
                        g * 32 : g * 32 + 32, c * 128 : c * 128 + 128
                    ]


def tail_of(values):
    row = lax.broadcasted_iota(jnp.int32, (16, 128), 0)
    tail = jnp.zeros((16, 128), f32)
    for k, value in enumerate(values):
        for p, piece in enumerate(split(value)):
            tail = jnp.where(row == 4 * p + k, piece.astype(f32), tail)
    return tail.astype(bf16)


def slopes_of(parts, pre, norms, loss, out):
    total = jnp.sum(parts[...].astype(f32), axis=0)
    for q in range(4):
        sums = []
        for c in range(3):
            k = q * 3 + c
            slope = total[k * 32 : k * 32 + 32] + (sparsity_weight / TOK_DEV) * norms[k : k + 1]
            slope = jnp.where(pre[k * 32 : k * 32 + 32] > 0, slope, 0.0)
            sums.append(jnp.sum(slope, axis=0, keepdims=True))
            for yh in range(2):
                out[yh * 4 + q, c * 32 : c * 32 + 32] = slope.astype(bf16)
        tail = tail_of([*sums, loss[0:1]])
        for yh in range(2):
            out[yh * 4 + q, 96:112] = tail


def regroup(got, out):
    tail = jnp.sum(got[:, 96:112].astype(f32), axis=0)
    tail = tail[0:4] + tail[4:8] + tail[8:12]
    tail = tail_of([tail[k : k + 1] for k in range(4)])
    for x in range(4):
        for m in range(8):
            out[x, m * 96 : m * 96 + 96] = got[m, 0:96]
        out[x, 768:784] = tail


def over_tokens(places, blocks, values, held, sems):
    copies = [pltpu.make_async_copy(blocks.at[q], held.at[q], sems.at[q]) for q in range(4)]
    for copy in copies:
        copy.start()
    total = None
    for q in range(4):
        copies[q].wait()
        halves = [
            jnp.concatenate([held[q, places[q, h * 8 + r]] for r in range(8)], axis=0)
            for h in range(2)
        ]
        wide = jnp.concatenate(halves, axis=1)
        column = lambda c: jnp.concatenate([values(h, q, c) for h in range(2)], axis=0)
        product = matmul(wide, jnp.concatenate([column(c) for c in range(3)], axis=1), 1, 0)
        total = product if total is None else total + product
    return total


def decoder_gradient(places, blocks, acts, rows, pull, reach, out, total, held, sems):
    values = lambda h, q, c: tokens_of(acts, h, q * 3 + c)
    total[...] = over_tokens(places, blocks, values, held, sems)
    for layer in range(LAYERS):
        for r in range(8):
            at = r * BLOCK + layer * 36
            out[layer, r * 36 : r * 36 + 36] = total[at : at + 36]
        whole = out[layer] + pull[0:1] * rows[layer].astype(f32)
        out[layer] = jnp.where(reach[layer : layer + 1] > 0, whole, 0.0)


def encoder_gradient(places, blocks, dpre, pick, out, bias, loss, total, held, sems):
    def values(half, q, c):
        parts = [
            dpre[half * 2 + g // 2, pl.ds(((g % 2) * 4 + q) * 96 + c * 32, 32)] for g in range(4)
        ]
        return jnp.concatenate(parts, axis=0)

    total[...] = over_tokens(places, blocks, values, held, sems)
    for r in range(8):
        own = jnp.zeros((36, 384), f32)
        for layer in range(LAYERS):
            at = r * BLOCK + layer * 36
            own = own + jnp.where(pick[layer : layer + 1] > 0, total[at : at + 36], 0.0)
        out[r * 36 : r * 36 + 36] = own
    tail = jnp.sum(dpre[:, 768:784].astype(f32), axis=0)
    tail = tail[0:4] + tail[4:8] + tail[8:12]
    bias[...] = tail[0:3]
    loss[...] = jnp.sum(tail[3:4], axis=1, keepdims=True) / TOK_DEV


def neighbour(block, axis):
    return lax.ppermute(block, axis, [(0, 1), (1, 0)])


def relative(blocks):
    yl, c = lax.axis_index("yl"), lax.axis_index("c")
    swapped = jnp.concatenate([blocks[2:], blocks[:2]])
    blocks = jnp.where(yl == 1, swapped, blocks)
    swapped = jnp.stack([blocks[1], blocks[0], blocks[3], blocks[2]])
    return jnp.where(c == 1, swapped, blocks)


together = lax.optimization_barrier


def on_device(resid, target, enc_weight, enc_bias, dec_weight, source):
    to = spread()
    back = [(d, s) for s, d in to]
    places = lax.dynamic_index_in_dim(
        jnp.array(PLACE, dtype=jnp.int32), lax.axis_index(DP), 0, False
    )
    at_z = lax.dynamic_index_in_dim(places, lax.axis_index(QUAD), 0, False)
    layer_ids = jnp.arange(LAYERS, dtype=jnp.int32)
    pick = source[None, :] == layer_ids[:, None]
    reach = source[None, :] <= layer_ids[:, None]

    both = jnp.stack([resid, target]).transpose(0, 2, 3, 1).reshape(2, 108, 128)
    both = jnp.pad(both, ((0, 0), (0, BLOCK - 108), (0, 0)))
    both = lax.ppermute(both, ALL, to)
    x_block, target_block = both[0], both[1]

    enc_t = enc_weight.T
    dec_t = jnp.where(reach[:, None, :], dec_weight.transpose(1, 2, 0), 0)
    square = jnp.sum(jnp.square(dec_t.astype(f32)), axis=(0, 1))
    dec_own = dec_t.reshape(3, 8, 36, 384).transpose(1, 0, 2, 3).reshape(8, 108, 384)
    dec_own = jnp.pad(dec_own, ((0, 0), (0, BLOCK - 108), (0, 0))).reshape(8 * BLOCK, 384)
    extra = jnp.stack([source.astype(bf16), *pieces(enc_bias), *pieces(square)])
    enc_own = jnp.concatenate([enc_t, jnp.pad(extra, ((0, 9), (0, 0)))])
    enc_quad = lax.all_gather(enc_own, QUAD)
    dec_quad = lax.all_gather(dec_own, QUAD)
    tail = enc_quad[:, 288:295].astype(f32)
    source_quad = tail[:, 0]
    bias_quad = (tail[:, 1] + tail[:, 2] + tail[:, 3]).reshape(1536)
    square_quad = (tail[:, 4] + tail[:, 5] + tail[:, 6]).reshape(1536)
    enc_rows = enc_quad[:, :288].reshape(4, 8, 1, 36, 384)
    pick_quad = source_quad[:, None, :] == layer_ids[None, :, None].astype(f32)
    enc_rows = jnp.where(pick_quad[:, None, :, None, :], enc_rows, 0).reshape(4, 8, 108, 384)
    enc_rows = jnp.pad(enc_rows, ((0, 0), (0, 0), (0, BLOCK - 108), (0, 0)))
    enc_rows = enc_rows.reshape(4, 8 * BLOCK, 384)

    x_quad = share(x_block, "z", 16)
    squares = jnp.pad(square_quad.reshape(12, 128), ((0, 4), (0, 0)))
    (partial,) = call(encode, at_z, x_quad, enc_rows, squares, out=[((8, 400, 128), f32)])
    partial = lax.all_to_all(partial, DP, 0, 0)
    partial, dec_quad = together((partial, dec_quad))
    pre, norms, acts, sparsity = call(
        activate,
        partial,
        bias_quad.reshape(12, 128),
        out=[((384, 128), f32), ((16, 128), f32), ((8, 384, 128), bf16), ((8, 128), f32)],
    )
    acts_quad = lax.all_to_all(acts, DP, 0, 0)

    (terms,) = call(decode, at_z, dec_quad, acts_quad, out=[((16, BLOCK, 128), bf16)])
    terms, acts_sent = together((terms, acts_quad))
    parts = lax.all_to_all(terms, "z", 0, 0)
    acts_sent = relative(acts_sent.reshape(8, 4, 96, 128).transpose(1, 0, 2, 3))
    near, far = acts_sent[:2], neighbour(acts_sent[2:], "yl")
    mine = jnp.stack([near[0], far[0]])
    other = neighbour(jnp.stack([near[1], far[1]]), "c")
    parts, mine, other = together((parts, mine, other))
    acts_every = relative(jnp.stack([mine[0], other[0], mine[1], other[1]]))
    acts_every = acts_every.transpose(1, 0, 2, 3).reshape(8, 384, 128)
    colsum = jnp.sum(acts_every.reshape(8, 4, 3, 32, 128).astype(f32), axis=(0, 1, 3)).reshape(384)
    recon, gout = call(
        compare,
        parts,
        target_block,
        sparsity,
        out=[((BLOCK, 128), bf16), ((16, BLOCK, 128), bf16)],
    )
    x_every = lax.all_gather(x_quad, QUAD)
    gout, x_every = together((gout, x_every))
    gout_all = lax.all_to_all(gout, "z", 0, 0)

    gout_every = lax.all_gather(gout_all, QUAD)
    slopes, loss_z = call(
        pull_back, at_z, gout_all, dec_quad, out=[((8, 384, 128), bf16), ((8, 128), f32)]
    )
    slopes = lax.all_to_all(slopes, DP, 0, 0)
    (sent,) = call(slopes_of, slopes, pre, norms, loss_z, out=[((8, 112, 128), bf16)])
    got = lax.all_to_all(sent, PLANE, 0, 0)
    (sent,) = call(regroup, got, out=[((4, 784, 128), bf16)])
    recon = lax.ppermute(recon, ALL, back)
    sent, recon = together((sent, recon))
    got = lax.all_to_all(sent, "x", 0, 0)

    scratch = [
        pltpu.VMEM((8 * BLOCK, 384), f32),
        pltpu.VMEM((4, 16, BLOCK, 128), bf16),
        pltpu.SemaphoreType.DMA((4,)),
    ]
    member = lax.axis_index(QUAD)
    own_norms = lax.dynamic_index_in_dim(norms[:12].reshape(4, 384), member, 0, False)
    pull = ((sparsity_weight / TOK_DEV) * colsum / own_norms)[None]
    (dec_grad,) = call(
        decoder_gradient,
        places,
        gout_every,
        acts_every,
        dec_t,
        pull,
        reach.astype(f32),
        out=[((LAYERS, 288, 384), f32)],
        scratch=scratch,
    )
    got, dec_grad = together((got, dec_grad))
    enc_grad, bias_grad, loss = call(
        encoder_gradient,
        places,
        x_every,
        got,
        pick.astype(f32),
        out=[((288, 384), f32), ((3, 128), f32), ((1, 1), f32)],
        scratch=scratch,
    )
    recon = recon[:108].reshape(3, 36, 128).transpose(2, 0, 1)
    return (loss[0, 0], recon, enc_grad.T, bias_grad.reshape(384), dec_grad.transpose(2, 0, 1))


def solution(mesh):
    fine = Mesh(np.asarray(mesh.devices).reshape(SIZES), ALL)
    in_specs = (
        P(DP, None, LATENT),
        P(DP, None, LATENT),
        P(LATENT, DP),
        P(LATENT),
        P(LATENT, None, DP),
        P(LATENT),
    )
    out_specs = (
        P(),
        P(DP, None, LATENT),
        P(LATENT, DP),
        P(LATENT),
        P(LATENT, None, DP),
    )
    return jax.shard_map(
        on_device, mesh=fine, in_specs=in_specs, out_specs=out_specs, check_vma=False
    )
```

```python
import jax
import jax.numpy as jnp
import numpy as np
from jax import lax
from jax.experimental import pallas as pl
from jax.experimental.pallas import tpu as pltpu
from jax.sharding import Mesh
from jax.sharding import PartitionSpec as P

LAYERS = 3
TOK_DEV = 128
SIZES = (4, 2, 16, 2, 2)
ALL = ("x", "yh", "z", "yl", "c")
DP = ("x", "yh")
LATENT = ("z", "yl", "c")
QUAD = ("yl", "c")
PLANE = ("yh", "yl", "c")
BLOCK = 112

sparsity_weight = 0.5
norm_epsilon = 1e-06
bf16, f32 = jnp.bfloat16, jnp.float32


PAIRS = ((0, 5), (1, 4), (2, 7), (3, 6))


def ring(a, b, size):
    return min((a - b) % size, (b - a) % size)


def placing(i, q):
    x, yh = divmod(i, 2)
    hops = []
    for a in PAIRS[q]:
        for r in range(8):
            beside = ring(a // 2, x, 4) + ring(2 * (a % 2) + r % 4 // 2, 2 * yh + q // 2, 4)
            hops.append([beside + ring(2 * i + r // 4, z, 16) for z in range(16)])

    def seat(block, seen):
        for z in range(16):
            if hops[block][z] <= most and z not in seen:
                seen.add(z)
                if owner[z] is None or seat(owner[z], seen):
                    owner[z] = block
                    return True
        return False

    for most in range(16):
        owner = [None] * 16
        if all(seat(block, set()) for block in range(16)):
            return [owner.index(block) for block in range(16)]


PLACE = [[placing(i, q) for q in range(4)] for i in range(8)]


def spread():
    pairs = []
    for i in range(8):
        for q in range(4):
            for block, z in enumerate(PLACE[i][q]):
                half, r = divmod(block, 8)
                pairs.append((PAIRS[q][half] * 64 + 8 * i + r, i * 64 + z * 4 + q))
    return pairs


def pieces(value):
    high = lax.reduce_precision(value, 8, 7)
    middle = lax.reduce_precision(value - high, 8, 7)
    low = value - high - middle
    return [high.astype(bf16), middle.astype(bf16), low.astype(bf16)]


def share(block, axes, count):
    return lax.all_to_all(jnp.broadcast_to(block[None], (count, *block.shape)), axes, 0, 0)


def call(kernel, *args, out, far=(), scratch=()):
    def place(k, arg):
        if arg.dtype == jnp.int32:
            return pl.BlockSpec(memory_space=pltpu.SMEM)
        return pl.BlockSpec(memory_space=pl.ANY if k in far else pltpu.VMEM)

    return pl.pallas_call(
        kernel,
        in_specs=[place(k, arg) for k, arg in enumerate(args)],
        out_shape=[jax.ShapeDtypeStruct(shape, dtype) for shape, dtype in out],
        scratch_shapes=scratch,
        compiler_params=pltpu.CompilerParams(vmem_limit_bytes=(56 if scratch else 40) * 2**20),
    )(*args)


ORDERED = [pltpu.VMEM((16 * BLOCK, 128), bf16), pltpu.SemaphoreType.DMA((16,))]
ROWS = [pltpu.VMEM((4, 8 * BLOCK, 384), bf16), pltpu.SemaphoreType.DMA((4,))]
EVERY = [
    pltpu.VMEM((8 * BLOCK, 384), f32),
    pltpu.VMEM((4, 16 * BLOCK, 128), bf16),
    pltpu.SemaphoreType.DMA((4, 16)),
]


def in_order(at_z, blocks, held, sems):
    copies = []
    for k in range(16):
        part = held.at[pl.ds(k * BLOCK, BLOCK)]
        copies.append(pltpu.make_async_copy(blocks.at[at_z(k)], part, sems.at[k]))
        copies[-1].start()
    return copies


def in_parts(rows, held, sems):
    copies = [pltpu.make_async_copy(rows.at[q], held.at[q], sems.at[q]) for q in range(4)]
    for copy in copies:
        copy.start()
    return copies


def split(value):
    high = value.astype(bf16)
    rest = value - high.astype(f32)
    middle = rest.astype(bf16)
    return [high, middle, (rest - middle.astype(f32)).astype(bf16)]


def matmul(a, b, left, right):
    return lax.dot_general(a, b, (((left,), (right,)), ((), ())), preferred_element_type=f32)


def encode(at_z, x, rows, squares, out, held, sems):
    copies = in_order(lambda k: at_z[k], x, held, sems)
    for half in range(2):
        for copy in copies[half * 8 : half * 8 + 8]:
            copy.wait()
        tokens = held[half * 8 * BLOCK : (half + 1) * 8 * BLOCK]
        for q in range(4):
            product = matmul(tokens, rows[q], 0, 0)
            for g in range(4):
                for c in range(3):
                    at = (q * 3 + c) * 32
                    out[half * 4 + g, at : at + 32] = product[
                        g * 32 : g * 32 + 32, c * 128 : c * 128 + 128
                    ]
    for g in range(8):
        out[g, 384:] = squares[...]


def activate(parts, bias, pre, norms, acts, sparsity):
    total = jnp.sum(parts[...], axis=0)
    norm = jnp.sqrt(total[384:396] + norm_epsilon)
    norms[0:12] = norm
    norms[12:16] = jnp.zeros((4, 128), f32)
    weighted = jnp.zeros((32, 128), f32)
    for c in range(12):
        here = total[c * 32 : c * 32 + 32] + bias[c : c + 1]
        pre[c * 32 : c * 32 + 32] = here
        low = jnp.maximum(here, 0.0).astype(bf16)
        weighted = weighted + low.astype(f32) * norm[c : c + 1]
        for g in range(8):
            acts[g, c * 32 : c * 32 + 32] = low
    sparsity[...] = jnp.broadcast_to(jnp.sum(weighted, axis=0, keepdims=True), (8, 128))


def tokens_of(ref, half, column):
    return ref[half * 4 : half * 4 + 4, column * 32 : column * 32 + 32].reshape(128, 128)


def decode(at_z, far_rows, acts, out, rows, sems):
    copies = in_parts(far_rows, rows, sems)
    totals = [None, None]
    for q in range(4):
        copies[q].wait()
        for half in range(2):
            wide = jnp.concatenate([tokens_of(acts, half, q * 3 + c) for c in range(3)], axis=1)
            product = matmul(rows[q], wide, 1, 1)
            totals[half] = product if q == 0 else totals[half] + product
    for half in range(2):
        low = totals[half].astype(bf16)
        for r in range(8):
            out[at_z[half * 8 + r]] = low[r * BLOCK : (r + 1) * BLOCK]


def compare(parts, target, sparsity, recon, gout):
    recon_sum = jnp.sum(parts[...].astype(f32), axis=0)
    recon[...] = recon_sum.astype(bf16)
    error = recon_sum - target[...].astype(f32)
    by_lane = jnp.sum(error * error, axis=0, keepdims=True) + sparsity_weight * sparsity[0:1]
    slope = 2.0 * error / TOK_DEV
    row = lax.broadcasted_iota(jnp.int32, (BLOCK, 128), 0)
    for k, piece in enumerate(split(by_lane)):
        slope = jnp.where(row == 108 + k, piece.astype(f32), slope)
    low = slope.astype(bf16)
    for z in range(16):
        gout[z] = low


def pull_back(at_z, gout, far_rows, out, loss, held, sems, rows, row_sems):
    copies = in_order(lambda k: at_z[k], gout, held, sems)
    row_copies = in_parts(far_rows, rows, row_sems)
    for copy in copies:
        copy.wait()
    total = jnp.zeros((16, 128), f32)
    for k in range(16):
        total = total + held[k * BLOCK + 96 : k * BLOCK + 112].astype(f32)
    loss[...] = jnp.broadcast_to(jnp.sum(total[12:15], axis=0, keepdims=True), (8, 128))
    for q in range(4):
        row_copies[q].wait()
        for half in range(2):
            tokens = held[half * 8 * BLOCK : (half + 1) * 8 * BLOCK]
            product = matmul(tokens, rows[q], 0, 0).astype(bf16)
            for g in range(4):
                for c in range(3):
                    at = (q * 3 + c) * 32
                    out[half * 4 + g, at : at + 32] = product[
                        g * 32 : g * 32 + 32, c * 128 : c * 128 + 128
                    ]


def tail_of(values):
    row = lax.broadcasted_iota(jnp.int32, (16, 128), 0)
    tail = jnp.zeros((16, 128), f32)
    for k, value in enumerate(values):
        for p, piece in enumerate(split(value)):
            tail = jnp.where(row == 4 * p + k, piece.astype(f32), tail)
    return tail.astype(bf16)


def slopes_of(parts, pre, norms, loss, out):
    total = jnp.sum(parts[...].astype(f32), axis=0)
    for q in range(4):
        sums = []
        for c in range(3):
            k = q * 3 + c
            slope = total[k * 32 : k * 32 + 32] + (sparsity_weight / TOK_DEV) * norms[k : k + 1]
            slope = jnp.where(pre[k * 32 : k * 32 + 32] > 0, slope, 0.0)
            sums.append(jnp.sum(slope, axis=0, keepdims=True))
            for yh in range(2):
                out[yh * 4 + q, c * 32 : c * 32 + 32] = slope.astype(bf16)
        tail = tail_of([*sums, loss[0:1]])
        for yh in range(2):
            out[yh * 4 + q, 96:112] = tail


def regroup(got, out):
    tail = jnp.sum(got[:, 96:112].astype(f32), axis=0)
    tail = tail[0:4] + tail[4:8] + tail[8:12]
    tail = tail_of([tail[k : k + 1] for k in range(4)])
    for x in range(4):
        for m in range(8):
            out[x, m * 96 : m * 96 + 96] = got[m, 0:96]
        out[x, 768:784] = tail


def over_tokens(places, blocks, values, held, sems):
    copies = [
        in_order(lambda k: places[q, k], blocks.at[q], held.at[q], sems.at[q]) for q in range(4)
    ]
    total = None
    for q in range(4):
        for copy in copies[q]:
            copy.wait()
        wide = jnp.concatenate([held[q, : 8 * BLOCK], held[q, 8 * BLOCK :]], axis=1)
        column = lambda c: jnp.concatenate([values(h, q, c) for h in range(2)], axis=0)
        product = matmul(wide, jnp.concatenate([column(c) for c in range(3)], axis=1), 1, 0)
        total = product if total is None else total + product
    return total


def decoder_gradient(places, blocks, acts, rows, pull, reach, out, total, held, sems):
    values = lambda h, q, c: tokens_of(acts, h, q * 3 + c)
    total[...] = over_tokens(places, blocks, values, held, sems)
    for layer in range(LAYERS):
        for r in range(8):
            at = r * BLOCK + layer * 36
            out[layer, r * 36 : r * 36 + 36] = total[at : at + 36]
        whole = out[layer] + pull[0:1] * rows[layer].astype(f32)
        out[layer] = jnp.where(reach[layer : layer + 1] > 0, whole, 0.0)


def encoder_gradient(places, blocks, dpre, pick, out, bias, loss, total, held, sems):
    def values(half, q, c):
        parts = [
            dpre[half * 2 + g // 2, pl.ds(((g % 2) * 4 + q) * 96 + c * 32, 32)] for g in range(4)
        ]
        return jnp.concatenate(parts, axis=0)

    total[...] = over_tokens(places, blocks, values, held, sems)
    for r in range(8):
        own = jnp.zeros((36, 384), f32)
        for layer in range(LAYERS):
            at = r * BLOCK + layer * 36
            own = own + jnp.where(pick[layer : layer + 1] > 0, total[at : at + 36], 0.0)
        out[r * 36 : r * 36 + 36] = own
    tail = jnp.sum(dpre[:, 768:784].astype(f32), axis=0)
    tail = tail[0:4] + tail[4:8] + tail[8:12]
    bias[...] = tail[0:3]
    loss[...] = jnp.sum(tail[3:4], axis=1, keepdims=True) / TOK_DEV


def neighbour(block, axis):
    return lax.ppermute(block, axis, [(0, 1), (1, 0)])


def relative(blocks):
    yl, c = lax.axis_index("yl"), lax.axis_index("c")
    swapped = jnp.concatenate([blocks[2:], blocks[:2]])
    blocks = jnp.where(yl == 1, swapped, blocks)
    swapped = jnp.stack([blocks[1], blocks[0], blocks[3], blocks[2]])
    return jnp.where(c == 1, swapped, blocks)


together = lax.optimization_barrier


def on_device(resid, target, enc_weight, enc_bias, dec_weight, source):
    to = spread()
    back = [(d, s) for s, d in to]
    places = lax.dynamic_index_in_dim(
        jnp.array(PLACE, dtype=jnp.int32), lax.axis_index(DP), 0, False
    )
    at_z = lax.dynamic_index_in_dim(places, lax.axis_index(QUAD), 0, False)
    layer_ids = jnp.arange(LAYERS, dtype=jnp.int32)
    pick = source[None, :] == layer_ids[:, None]
    reach = source[None, :] <= layer_ids[:, None]

    both = jnp.stack([resid, target]).transpose(0, 2, 3, 1).reshape(2, 108, 128)
    both = jnp.pad(both, ((0, 0), (0, BLOCK - 108), (0, 0)))
    both = lax.ppermute(both, ALL, to)
    x_block, target_block = both[0], both[1]

    enc_t = enc_weight.T
    dec_t = jnp.where(reach[:, None, :], dec_weight.transpose(1, 2, 0), 0)
    square = jnp.sum(jnp.square(dec_t.astype(f32)), axis=(0, 1))
    dec_own = dec_t.reshape(3, 8, 36, 384).transpose(1, 0, 2, 3).reshape(8, 108, 384)
    dec_own = jnp.pad(dec_own, ((0, 0), (0, BLOCK - 108), (0, 0))).reshape(8 * BLOCK, 384)
    extra = jnp.stack([source.astype(bf16), *pieces(enc_bias), *pieces(square)])
    enc_own = jnp.concatenate([enc_t, jnp.pad(extra, ((0, 9), (0, 0)))])
    enc_quad = lax.all_gather(enc_own, QUAD)
    dec_quad = lax.all_gather(dec_own, QUAD)
    tail = enc_quad[:, 288:295].astype(f32)
    source_quad = tail[:, 0]
    bias_quad = (tail[:, 1] + tail[:, 2] + tail[:, 3]).reshape(1536)
    square_quad = (tail[:, 4] + tail[:, 5] + tail[:, 6]).reshape(1536)
    enc_rows = enc_quad[:, :288].reshape(4, 8, 1, 36, 384)
    pick_quad = source_quad[:, None, :] == layer_ids[None, :, None].astype(f32)
    enc_rows = jnp.where(pick_quad[:, None, :, None, :], enc_rows, 0).reshape(4, 8, 108, 384)
    enc_rows = jnp.pad(enc_rows, ((0, 0), (0, 0), (0, BLOCK - 108), (0, 0)))
    enc_rows = enc_rows.reshape(4, 8 * BLOCK, 384)

    x_quad = share(x_block, "z", 16)
    squares = jnp.pad(square_quad.reshape(12, 128), ((0, 4), (0, 0)))
    (partial,) = call(
        encode,
        at_z,
        x_quad,
        enc_rows,
        squares,
        out=[((8, 400, 128), f32)],
        far=(1,),
        scratch=ORDERED,
    )
    partial = lax.all_to_all(partial, DP, 0, 0)
    pre, norms, acts, sparsity = call(
        activate,
        partial,
        bias_quad.reshape(12, 128),
        out=[((384, 128), f32), ((16, 128), f32), ((8, 384, 128), bf16), ((8, 128), f32)],
    )
    acts_quad = lax.all_to_all(acts, DP, 0, 0)

    (terms,) = call(
        decode,
        at_z,
        dec_quad,
        acts_quad,
        out=[((16, BLOCK, 128), bf16)],
        far=(1,),
        scratch=ROWS,
    )
    terms, acts_sent = together((terms, acts_quad))
    parts = lax.all_to_all(terms, "z", 0, 0)
    acts_sent = relative(acts_sent.reshape(8, 4, 96, 128).transpose(1, 0, 2, 3))
    near, far = acts_sent[:2], neighbour(acts_sent[2:], "yl")
    mine = jnp.stack([near[0], far[0]])
    other = neighbour(jnp.stack([near[1], far[1]]), "c")
    parts, mine, other, x_sent = together((parts, mine, other, x_quad))
    acts_every = relative(jnp.stack([mine[0], other[0], mine[1], other[1]]))
    acts_every = acts_every.transpose(1, 0, 2, 3).reshape(8, 384, 128)
    colsum = jnp.sum(acts_every.reshape(8, 4, 3, 32, 128).astype(f32), axis=(0, 1, 3)).reshape(384)
    recon, gout = call(
        compare,
        parts,
        target_block,
        sparsity,
        out=[((BLOCK, 128), bf16), ((16, BLOCK, 128), bf16)],
    )
    x_every = lax.all_gather(x_sent, QUAD)
    gout_all = lax.all_to_all(gout, "z", 0, 0)

    gout_sent, x_every = together((gout_all, x_every))
    gout_every = lax.all_gather(gout_sent, QUAD)
    slopes, loss_z = call(
        pull_back,
        at_z,
        gout_all,
        dec_quad,
        out=[((8, 384, 128), bf16), ((8, 128), f32)],
        far=(1, 2),
        scratch=ORDERED + ROWS,
    )
    slopes = lax.all_to_all(slopes, DP, 0, 0)
    (sent,) = call(slopes_of, slopes, pre, norms, loss_z, out=[((8, 112, 128), bf16)])
    got = lax.all_to_all(sent, PLANE, 0, 0)
    (sent,) = call(regroup, got, out=[((4, 784, 128), bf16)])
    recon = lax.ppermute(recon, ALL, back)
    sent, recon = together((sent, recon))
    got = lax.all_to_all(sent, "x", 0, 0)

    member = lax.axis_index(QUAD)
    own_norms = lax.dynamic_index_in_dim(norms[:12].reshape(4, 384), member, 0, False)
    pull = ((sparsity_weight / TOK_DEV) * colsum / own_norms)[None]
    (dec_grad,) = call(
        decoder_gradient,
        places,
        gout_every,
        acts_every,
        dec_t,
        pull,
        reach.astype(f32),
        out=[((LAYERS, 288, 384), f32)],
        far=(1,),
        scratch=EVERY,
    )
    got, dec_grad = together((got, dec_grad))
    enc_grad, bias_grad, loss = call(
        encoder_gradient,
        places,
        x_every,
        got,
        pick.astype(f32),
        out=[((288, 384), f32), ((3, 128), f32), ((1, 1), f32)],
        far=(1,),
        scratch=EVERY,
    )
    recon = recon[:108].reshape(3, 36, 128).transpose(2, 0, 1)
    return (loss[0, 0], recon, enc_grad.T, bias_grad.reshape(384), dec_grad.transpose(2, 0, 1))


def solution(mesh):
    fine = Mesh(np.asarray(mesh.devices).reshape(SIZES), ALL)
    in_specs = (
        P(DP, None, LATENT),
        P(DP, None, LATENT),
        P(LATENT, DP),
        P(LATENT),
        P(LATENT, None, DP),
        P(LATENT),
    )
    out_specs = (
        P(),
        P(DP, None, LATENT),
        P(LATENT, DP),
        P(LATENT),
        P(LATENT, None, DP),
    )
    return jax.shard_map(
        on_device, mesh=fine, in_specs=in_specs, out_specs=out_specs, check_vma=False
    )
```

```python
import jax
import jax.numpy as jnp
import numpy as np
from jax import lax
from jax.experimental import pallas as pl
from jax.experimental.pallas import tpu as pltpu
from jax.sharding import Mesh
from jax.sharding import PartitionSpec as P

LAYERS = 3
TOK_DEV = 128
SIZES = (4, 2, 16, 2, 2)
ALL = ("x", "yh", "z", "yl", "c")
DP = ("x", "yh")
LATENT = ("z", "yl", "c")
QUAD = ("yl", "c")
PLANE = ("yh", "yl", "c")
BLOCK = 112

sparsity_weight = 0.5
norm_epsilon = 1e-06
bf16, f32 = jnp.bfloat16, jnp.float32


def spread():
    pairs = []
    for a in range(8):
        for b in range(64):
            i, r = divmod(b, 8)
            pairs.append((a * 64 + b, i * 64 + ((a % 2) * 8 + r) * 4 + a // 2))
    return pairs


def pieces(value):
    high = lax.reduce_precision(value, 8, 7)
    middle = lax.reduce_precision(value - high, 8, 7)
    low = value - high - middle
    return [high.astype(bf16), middle.astype(bf16), low.astype(bf16)]


def share(block, axes, count):
    return lax.all_to_all(jnp.broadcast_to(block[None], (count, *block.shape)), axes, 0, 0)


def call(kernel, *args, out, scratch=()):
    return pl.pallas_call(
        kernel,
        out_shape=[jax.ShapeDtypeStruct(shape, dtype) for shape, dtype in out],
        scratch_shapes=scratch,
        compiler_params=pltpu.CompilerParams(vmem_limit_bytes=40 * 1024 * 1024),
    )(*args)


def split(value):
    high = value.astype(bf16)
    rest = value - high.astype(f32)
    middle = rest.astype(bf16)
    return [high, middle, (rest - middle.astype(f32)).astype(bf16)]


def matmul(a, b, left, right):
    return lax.dot_general(a, b, (((left,), (right,)), ((), ())), preferred_element_type=f32)


def arrange(dec, reach, out, square, masked, ordered):
    total = jnp.zeros((1, 384), f32)
    for layer in range(LAYERS):
        masked[...] = jnp.where(reach[layer : layer + 1] > 0, dec[layer].astype(f32), 0.0)
        total = total + jnp.sum(masked[...] * masked[...], axis=0, keepdims=True)
        for r in range(8):
            at = r * BLOCK + layer * 36
            ordered[at : at + 36] = masked[r * 36 : r * 36 + 36]
    for r in range(8):
        ordered[r * BLOCK + 108 : (r + 1) * BLOCK] = jnp.zeros((BLOCK - 108, 384), f32)
    out[...] = ordered[...].astype(bf16)
    square[...] = total


def encode(x, rows, squares, out):
    for half in range(2):
        for q in range(4):
            product = matmul(x[half], rows[q], 0, 0)
            for g in range(4):
                for c in range(3):
                    at = (q * 3 + c) * 32
                    out[half * 4 + g, at : at + 32] = product[
                        g * 32 : g * 32 + 32, c * 128 : c * 128 + 128
                    ]
    for g in range(8):
        out[g, 384:] = squares[...]


def activate(parts, bias, pre, norms, acts, sparsity):
    total = jnp.sum(parts[...], axis=0)
    norm = jnp.sqrt(total[384:396] + norm_epsilon)
    norms[0:12] = norm
    norms[12:16] = jnp.zeros((4, 128), f32)
    weighted = jnp.zeros((32, 128), f32)
    for c in range(12):
        here = total[c * 32 : c * 32 + 32] + bias[c : c + 1]
        pre[c * 32 : c * 32 + 32] = here
        low = jnp.maximum(here, 0.0).astype(bf16)
        weighted = weighted + low.astype(f32) * norm[c : c + 1]
        for g in range(8):
            acts[g, c * 32 : c * 32 + 32] = low
    sparsity[...] = jnp.broadcast_to(jnp.sum(weighted, axis=0, keepdims=True), (8, 128))


def tokens_of(ref, half, column):
    return ref[half * 4 : half * 4 + 4, column * 32 : column * 32 + 32].reshape(128, 128)


def decode(rows, acts, out):
    for half in range(2):
        total = None
        for q in range(4):
            wide = jnp.concatenate([tokens_of(acts, half, q * 3 + c) for c in range(3)], axis=1)
            product = matmul(rows[q], wide, 1, 1)
            total = product if total is None else total + product
        low = total.astype(bf16)
        for r in range(8):
            out[half * 8 + r] = low[r * BLOCK : (r + 1) * BLOCK]


def compare(parts, target, sparsity, recon, gout):
    recon_sum = jnp.sum(parts[...].astype(f32), axis=0)
    recon[...] = recon_sum.astype(bf16)
    error = recon_sum - target[...].astype(f32)
    by_lane = jnp.sum(error * error, axis=0, keepdims=True) + sparsity_weight * sparsity[0:1]
    slope = 2.0 * error / TOK_DEV
    row = lax.broadcasted_iota(jnp.int32, (BLOCK, 128), 0)
    for k, piece in enumerate(split(by_lane)):
        slope = jnp.where(row == 108 + k, piece.astype(f32), slope)
    low = slope.astype(bf16)
    for z in range(16):
        gout[z] = low


def pull_back(gout, rows, out, loss):
    total = jnp.sum(gout[:, 96:112].astype(f32), axis=0)
    loss[...] = jnp.broadcast_to(jnp.sum(total[12:15], axis=0, keepdims=True), (8, 128))
    for half in range(2):
        tokens = jnp.concatenate([gout[half * 8 + r] for r in range(8)], axis=0)
        for q in range(4):
            product = matmul(tokens, rows[q], 0, 0).astype(bf16)
            for g in range(4):
                for c in range(3):
                    at = (q * 3 + c) * 32
                    out[half * 4 + g, at : at + 32] = product[
                        g * 32 : g * 32 + 32, c * 128 : c * 128 + 128
                    ]


def tail_of(values):
    row = lax.broadcasted_iota(jnp.int32, (16, 128), 0)
    tail = jnp.zeros((16, 128), f32)
    for k, value in enumerate(values):
        for p, piece in enumerate(split(value)):
            tail = jnp.where(row == 4 * p + k, piece.astype(f32), tail)
    return tail.astype(bf16)


def slopes_of(parts, pre, norms, loss, out):
    total = jnp.sum(parts[...].astype(f32), axis=0)
    for q in range(4):
        sums = []
        for c in range(3):
            k = q * 3 + c
            slope = total[k * 32 : k * 32 + 32] + (sparsity_weight / TOK_DEV) * norms[k : k + 1]
            slope = jnp.where(pre[k * 32 : k * 32 + 32] > 0, slope, 0.0)
            sums.append(jnp.sum(slope, axis=0, keepdims=True))
            for yh in range(2):
                out[yh * 4 + q, c * 32 : c * 32 + 32] = slope.astype(bf16)
        tail = tail_of([*sums, loss[0:1]])
        for yh in range(2):
            out[yh * 4 + q, 96:112] = tail


def regroup(got, out):
    tail = jnp.sum(got[:, 96:112].astype(f32), axis=0)
    tail = tail[0:4] + tail[4:8] + tail[8:12]
    tail = tail_of([tail[k : k + 1] for k in range(4)])
    for x in range(4):
        for m in range(8):
            out[x, m * 96 : m * 96 + 96] = got[m, 0:96]
        out[x, 768:784] = tail


def over_tokens(blocks, values):
    total = None
    for q in range(4):
        wide = jnp.concatenate([blocks[q, 0], blocks[q, 1]], axis=1)
        column = lambda c: jnp.concatenate([values(h, q, c) for h in range(2)], axis=0)
        product = matmul(wide, jnp.concatenate([column(c) for c in range(3)], axis=1), 1, 0)
        total = product if total is None else total + product
    return total


def decoder_gradient(blocks, acts, rows, norms, reach, out, total):
    def values(half, q, c):
        here = acts[q, half * 4 : half * 4 + 4, c * 32 : c * 32 + 32]
        return here.reshape(128, 128)

    total[...] = over_tokens(blocks, values)
    sums = []
    for c in range(3):
        column = acts[:, :, c * 32 : c * 32 + 32].reshape(1024, 128).astype(f32)
        sums.append(jnp.sum(column, axis=0, keepdims=True))
    pull = (sparsity_weight / TOK_DEV) * jnp.concatenate(sums, axis=1) / norms[...]
    for layer in range(LAYERS):
        for r in range(8):
            at = r * BLOCK + layer * 36
            out[layer, r * 36 : r * 36 + 36] = total[at : at + 36]
        whole = out[layer] + pull * rows[layer].astype(f32)
        out[layer] = jnp.where(reach[layer : layer + 1] > 0, whole, 0.0)


def encoder_gradient(blocks, dpre, pick, out, bias, loss, total):
    def values(half, q, c):
        parts = [
            dpre[half * 2 + g // 2, pl.ds(((g % 2) * 4 + q) * 96 + c * 32, 32)] for g in range(4)
        ]
        return jnp.concatenate(parts, axis=0)

    total[...] = over_tokens(blocks, values)
    for r in range(8):
        own = jnp.zeros((36, 384), f32)
        for layer in range(LAYERS):
            at = r * BLOCK + layer * 36
            own = own + jnp.where(pick[layer : layer + 1] > 0, total[at : at + 36], 0.0)
        out[r * 36 : r * 36 + 36] = own
    tail = jnp.sum(dpre[:, 768:784].astype(f32), axis=0)
    tail = tail[0:4] + tail[4:8] + tail[8:12]
    bias[...] = tail[0:3]
    loss[...] = jnp.sum(tail[3:4], axis=1, keepdims=True) / TOK_DEV


together = lax.optimization_barrier


def on_device(resid, target, enc_weight, enc_bias, dec_weight, source):
    to = spread()
    back = [(d, s) for s, d in to]
    layer_ids = jnp.arange(LAYERS, dtype=jnp.int32)
    pick = source[None, :] == layer_ids[:, None]
    reach = source[None, :] <= layer_ids[:, None]

    both = jnp.stack([resid, target]).transpose(0, 2, 3, 1).reshape(2, 108, 128)
    both = jnp.pad(both, ((0, 0), (0, BLOCK - 108), (0, 0)))
    both = lax.ppermute(both, ALL, to)
    x_block, target_block = both[0], both[1]

    enc_t = enc_weight.T
    dec_t = dec_weight.transpose(1, 2, 0)
    reach_wide = reach.astype(f32)
    dec_own, square = call(
        arrange,
        dec_t,
        reach_wide,
        out=[((8 * BLOCK, 384), bf16), ((1, 384), f32)],
        scratch=[pltpu.VMEM((288, 384), f32), pltpu.VMEM((8 * BLOCK, 384), f32)],
    )
    extra = jnp.stack([source.astype(bf16), *pieces(enc_bias), *pieces(square[0])])
    enc_own = jnp.concatenate([enc_t, jnp.pad(extra, ((0, 9), (0, 0)))])
    enc_quad = lax.all_gather(enc_own, QUAD)
    dec_quad = lax.all_gather(dec_own, QUAD)
    tail = enc_quad[:, 288:295].astype(f32)
    source_quad = tail[:, 0]
    bias_quad = (tail[:, 1] + tail[:, 2] + tail[:, 3]).reshape(1536)
    square_quad = (tail[:, 4] + tail[:, 5] + tail[:, 6]).reshape(1536)
    enc_rows = enc_quad[:, :288].reshape(4, 8, 1, 36, 384)
    pick_quad = source_quad[:, None, :] == layer_ids[None, :, None].astype(f32)
    enc_rows = jnp.where(pick_quad[:, None, :, None, :], enc_rows, 0).reshape(4, 8, 108, 384)
    enc_rows = jnp.pad(enc_rows, ((0, 0), (0, 0), (0, BLOCK - 108), (0, 0)))
    enc_rows = enc_rows.reshape(4, 8 * BLOCK, 384)

    x_quad = share(x_block, "z", 16).reshape(2, 8 * BLOCK, 128)
    squares = jnp.pad(square_quad.reshape(12, 128), ((0, 4), (0, 0)))
    (partial,) = call(encode, x_quad, enc_rows, squares, out=[((8, 400, 128), f32)])
    partial = lax.all_to_all(partial, DP, 0, 0)
    pre, norms, acts, sparsity = call(
        activate,
        partial,
        bias_quad.reshape(12, 128),
        out=[((384, 128), f32), ((16, 128), f32), ((8, 384, 128), bf16), ((8, 128), f32)],
    )
    acts, dec_quad = together((acts, dec_quad))
    acts_quad = lax.all_to_all(acts, DP, 0, 0)

    (terms,) = call(decode, dec_quad, acts_quad, out=[((16, BLOCK, 128), bf16)])
    parts = lax.all_to_all(terms, "z", 0, 0)
    acts_every = lax.all_gather(acts_quad, QUAD)
    member = lax.axis_index(QUAD)
    acts_every = lax.dynamic_slice_in_dim(acts_every, member * 96, 96, 2)
    recon, gout = call(
        compare,
        parts,
        target_block,
        sparsity,
        out=[((BLOCK, 128), bf16), ((16, BLOCK, 128), bf16)],
    )
    x_every = lax.all_gather(x_quad, QUAD)
    gout, x_every = together((gout, x_every))
    gout_all = lax.all_to_all(gout, "z", 0, 0)

    gout_every = lax.all_gather(gout_all.reshape(2, 8 * BLOCK, 128), QUAD)
    slopes, loss_z = call(
        pull_back, gout_all, dec_quad, out=[((8, 384, 128), bf16), ((8, 128), f32)]
    )
    slopes = lax.all_to_all(slopes, DP, 0, 0)
    (sent,) = call(slopes_of, slopes, pre, norms, loss_z, out=[((8, 112, 128), bf16)])
    got = lax.all_to_all(sent, PLANE, 0, 0)
    (sent,) = call(regroup, got, out=[((4, 784, 128), bf16)])
    recon = lax.ppermute(recon, ALL, back)
    sent, recon = together((sent, recon))
    got = lax.all_to_all(sent, "x", 0, 0)

    total = pltpu.VMEM((8 * BLOCK, 384), f32)
    own_norms = lax.dynamic_index_in_dim(norms[:12].reshape(4, 384), member, 0, True)
    (dec_grad,) = call(
        decoder_gradient,
        gout_every,
        acts_every,
        dec_t,
        own_norms,
        reach_wide,
        out=[((LAYERS, 288, 384), f32)],
        scratch=[total],
    )
    got, dec_grad = together((got, dec_grad))
    enc_grad, bias_grad, loss = call(
        encoder_gradient,
        x_every,
        got,
        pick.astype(f32),
        out=[((288, 384), f32), ((3, 128), f32), ((1, 1), f32)],
        scratch=[total],
    )
    recon = recon[:108].reshape(3, 36, 128).transpose(2, 0, 1)
    return (loss[0, 0], recon, enc_grad.T, bias_grad.reshape(384), dec_grad.transpose(2, 0, 1))


def solution(mesh):
    fine = Mesh(np.asarray(mesh.devices).reshape(SIZES), ALL)
    in_specs = (
        P(DP, None, LATENT),
        P(DP, None, LATENT),
        P(LATENT, DP),
        P(LATENT),
        P(LATENT, None, DP),
        P(LATENT),
    )
    out_specs = (
        P(),
        P(DP, None, LATENT),
        P(LATENT, DP),
        P(LATENT),
        P(LATENT, None, DP),
    )
    return jax.shard_map(
        on_device, mesh=fine, in_specs=in_specs, out_specs=out_specs, check_vma=False
    )
```

```python
import jax
import jax.numpy as jnp
import numpy as np
from jax import lax
from jax.experimental import pallas as pl
from jax.experimental.pallas import tpu as pltpu
from jax.sharding import Mesh
from jax.sharding import PartitionSpec as P

LAYERS = 3
TOK_DEV = 128
SIZES = (4, 2, 16, 2, 2)
ALL = ("x", "yh", "z", "yl", "c")
DP = ("x", "yh")
LATENT = ("z", "yl", "c")
QUAD = ("yl", "c")
PLANE = ("yh", "yl", "c")
BLOCK = 112

sparsity_weight = 0.5
norm_epsilon = 1e-06
bf16, f32 = jnp.bfloat16, jnp.float32


def spread():
    pairs = []
    for a in range(8):
        for b in range(64):
            i, r = divmod(b, 8)
            pairs.append((a * 64 + b, i * 64 + ((a % 2) * 8 + r) * 4 + a // 2))
    return pairs


def pieces(value):
    high = lax.reduce_precision(value, 8, 7)
    middle = lax.reduce_precision(value - high, 8, 7)
    low = value - high - middle
    return [high.astype(bf16), middle.astype(bf16), low.astype(bf16)]


def share(block, axes, count):
    return lax.all_to_all(jnp.broadcast_to(block[None], (count, *block.shape)), axes, 0, 0)


def call(kernel, *args, out, scratch=()):
    return pl.pallas_call(
        kernel,
        out_shape=[jax.ShapeDtypeStruct(shape, dtype) for shape, dtype in out],
        scratch_shapes=scratch,
        compiler_params=pltpu.CompilerParams(vmem_limit_bytes=40 * 1024 * 1024),
    )(*args)


def split(value):
    high = value.astype(bf16)
    rest = value - high.astype(f32)
    middle = rest.astype(bf16)
    return [high, middle, (rest - middle.astype(f32)).astype(bf16)]


def matmul(a, b, left, right):
    return lax.dot_general(a, b, (((left,), (right,)), ((), ())), preferred_element_type=f32)


def arrange(dec, reach, out, square, masked, ordered):
    total = jnp.zeros((1, 384), f32)
    for layer in range(LAYERS):
        masked[...] = jnp.where(reach[layer : layer + 1] > 0, dec[layer].astype(f32), 0.0)
        total = total + jnp.sum(masked[...] * masked[...], axis=0, keepdims=True)
        for r in range(8):
            at = r * BLOCK + layer * 36
            ordered[at : at + 36] = masked[r * 36 : r * 36 + 36]
    for r in range(8):
        ordered[r * BLOCK + 108 : (r + 1) * BLOCK] = jnp.zeros((BLOCK - 108, 384), f32)
    out[...] = ordered[...].astype(bf16)
    square[...] = total


def encode(x, rows, sources, squares, out, wide, by_layer):
    wide[...] = x[...].reshape(16 * BLOCK, 128).astype(f32)
    for half in range(2):
        for layer in range(LAYERS):
            for r in range(8):
                at = (half * 8 + r) * BLOCK + layer * 36
                by_layer[half, layer, r * 36 : r * 36 + 36] = wide[at : at + 36]
    for half in range(2):
        tokens = [by_layer[half, layer].astype(bf16) for layer in range(LAYERS)]
        for q in range(4):
            product = jnp.zeros((128, 384), f32)
            for layer in range(LAYERS):
                here = matmul(tokens[layer], rows[q, 0:288], 0, 0)
                product = product + jnp.where(sources[q : q + 1] == layer, here, 0.0)
            for g in range(4):
                for c in range(3):
                    at = (q * 3 + c) * 32
                    out[half * 4 + g, at : at + 32] = product[
                        g * 32 : g * 32 + 32, c * 128 : c * 128 + 128
                    ]
    for g in range(8):
        out[g, 384:] = squares[...]


def activate(parts, bias, pre, norms, acts, sparsity):
    total = jnp.sum(parts[...], axis=0)
    norm = jnp.sqrt(total[384:396] + norm_epsilon)
    norms[0:12] = norm
    norms[12:16] = jnp.zeros((4, 128), f32)
    weighted = jnp.zeros((32, 128), f32)
    for c in range(12):
        here = total[c * 32 : c * 32 + 32] + bias[c : c + 1]
        pre[c * 32 : c * 32 + 32] = here
        low = jnp.maximum(here, 0.0).astype(bf16)
        weighted = weighted + low.astype(f32) * norm[c : c + 1]
        for g in range(8):
            acts[g, c * 32 : c * 32 + 32] = low
    sparsity[...] = jnp.broadcast_to(jnp.sum(weighted, axis=0, keepdims=True), (8, 128))


def tokens_of(ref, half, column):
    return ref[half * 4 : half * 4 + 4, column * 32 : column * 32 + 32].reshape(128, 128)


def decode(rows, acts, out):
    for half in range(2):
        total = None
        for q in range(4):
            wide = jnp.concatenate([tokens_of(acts, half, q * 3 + c) for c in range(3)], axis=1)
            product = matmul(rows[q], wide, 1, 1)
            total = product if total is None else total + product
        low = total.astype(bf16)
        for r in range(8):
            out[half * 8 + r] = low[r * BLOCK : (r + 1) * BLOCK]


def compare(parts, target, sparsity, recon, gout):
    recon_sum = jnp.sum(parts[...].astype(f32), axis=0)
    recon[...] = recon_sum.astype(bf16)
    error = recon_sum - target[...].astype(f32)
    by_lane = jnp.sum(error * error, axis=0, keepdims=True) + sparsity_weight * sparsity[0:1]
    slope = 2.0 * error / TOK_DEV
    row = lax.broadcasted_iota(jnp.int32, (BLOCK, 128), 0)
    for k, piece in enumerate(split(by_lane)):
        slope = jnp.where(row == 108 + k, piece.astype(f32), slope)
    low = slope.astype(bf16)
    for z in range(16):
        gout[z] = low


def pull_back(gout, rows, out, loss):
    total = jnp.sum(gout[:, 96:112].astype(f32), axis=0)
    loss[...] = jnp.broadcast_to(jnp.sum(total[12:15], axis=0, keepdims=True), (8, 128))
    for half in range(2):
        tokens = jnp.concatenate([gout[half * 8 + r] for r in range(8)], axis=0)
        for q in range(4):
            product = matmul(tokens, rows[q], 0, 0).astype(bf16)
            for g in range(4):
                for c in range(3):
                    at = (q * 3 + c) * 32
                    out[half * 4 + g, at : at + 32] = product[
                        g * 32 : g * 32 + 32, c * 128 : c * 128 + 128
                    ]


def tail_of(values):
    row = lax.broadcasted_iota(jnp.int32, (16, 128), 0)
    tail = jnp.zeros((16, 128), f32)
    for k, value in enumerate(values):
        for p, piece in enumerate(split(value)):
            tail = jnp.where(row == 4 * p + k, piece.astype(f32), tail)
    return tail.astype(bf16)


def slopes_of(parts, pre, norms, loss, out):
    total = jnp.sum(parts[...].astype(f32), axis=0)
    for q in range(4):
        sums = []
        for c in range(3):
            k = q * 3 + c
            slope = total[k * 32 : k * 32 + 32] + (sparsity_weight / TOK_DEV) * norms[k : k + 1]
            slope = jnp.where(pre[k * 32 : k * 32 + 32] > 0, slope, 0.0)
            sums.append(jnp.sum(slope, axis=0, keepdims=True))
            for yh in range(2):
                out[yh * 4 + q, c * 32 : c * 32 + 32] = slope.astype(bf16)
        tail = tail_of([*sums, loss[0:1]])
        for yh in range(2):
            out[yh * 4 + q, 96:112] = tail


def regroup(got, out):
    tail = jnp.sum(got[:, 96:112].astype(f32), axis=0)
    tail = tail[0:4] + tail[4:8] + tail[8:12]
    tail = tail_of([tail[k : k + 1] for k in range(4)])
    for x in range(4):
        for m in range(8):
            out[x, m * 96 : m * 96 + 96] = got[m, 0:96]
        out[x, 768:784] = tail


def over_tokens(blocks, values):
    total = None
    for q in range(4):
        wide = jnp.concatenate([blocks[q, 0], blocks[q, 1]], axis=1)
        column = lambda c: jnp.concatenate([values(h, q, c) for h in range(2)], axis=0)
        product = matmul(wide, jnp.concatenate([column(c) for c in range(3)], axis=1), 1, 0)
        total = product if total is None else total + product
    return total


def decoder_gradient(blocks, acts, rows, norms, reach, out, total):
    def values(half, q, c):
        here = acts[q, half * 4 : half * 4 + 4, c * 32 : c * 32 + 32]
        return here.reshape(128, 128)

    total[...] = over_tokens(blocks, values)
    sums = []
    for c in range(3):
        column = acts[:, :, c * 32 : c * 32 + 32].reshape(1024, 128).astype(f32)
        sums.append(jnp.sum(column, axis=0, keepdims=True))
    pull = (sparsity_weight / TOK_DEV) * jnp.concatenate(sums, axis=1) / norms[...]
    for layer in range(LAYERS):
        for r in range(8):
            at = r * BLOCK + layer * 36
            out[layer, r * 36 : r * 36 + 36] = total[at : at + 36]
        whole = out[layer] + pull * rows[layer].astype(f32)
        out[layer] = jnp.where(reach[layer : layer + 1] > 0, whole, 0.0)


def encoder_gradient(blocks, dpre, pick, out, bias, loss, total):
    def values(half, q, c):
        parts = [
            dpre[half * 2 + g // 2, pl.ds(((g % 2) * 4 + q) * 96 + c * 32, 32)] for g in range(4)
        ]
        return jnp.concatenate(parts, axis=0)

    total[...] = over_tokens(blocks, values)
    for r in range(8):
        own = jnp.zeros((36, 384), f32)
        for layer in range(LAYERS):
            at = r * BLOCK + layer * 36
            own = own + jnp.where(pick[layer : layer + 1] > 0, total[at : at + 36], 0.0)
        out[r * 36 : r * 36 + 36] = own
    tail = jnp.sum(dpre[:, 768:784].astype(f32), axis=0)
    tail = tail[0:4] + tail[4:8] + tail[8:12]
    bias[...] = tail[0:3]
    loss[...] = jnp.sum(tail[3:4], axis=1, keepdims=True) / TOK_DEV


together = lax.optimization_barrier


def on_device(resid, target, enc_weight, enc_bias, dec_weight, source):
    to = spread()
    back = [(d, s) for s, d in to]
    layer_ids = jnp.arange(LAYERS, dtype=jnp.int32)
    pick = source[None, :] == layer_ids[:, None]
    reach = source[None, :] <= layer_ids[:, None]

    both = jnp.stack([resid, target]).transpose(0, 2, 3, 1).reshape(2, 108, 128)
    both = jnp.pad(both, ((0, 0), (0, BLOCK - 108), (0, 0)))
    both = lax.ppermute(both, ALL, to)
    x_block, target_block = both[0], both[1]

    enc_t = enc_weight.T
    dec_t = dec_weight.transpose(1, 2, 0)
    reach_wide = reach.astype(f32)
    dec_own, square = call(
        arrange,
        dec_t,
        reach_wide,
        out=[((8 * BLOCK, 384), bf16), ((1, 384), f32)],
        scratch=[pltpu.VMEM((288, 384), f32), pltpu.VMEM((8 * BLOCK, 384), f32)],
    )
    extra = jnp.stack([source.astype(bf16), *pieces(enc_bias), *pieces(square[0])])
    enc_own = jnp.concatenate([enc_t, jnp.pad(extra, ((0, 9), (0, 0)))])
    enc_quad = lax.all_gather(enc_own, QUAD)
    dec_quad = lax.all_gather(dec_own, QUAD)
    tail = enc_quad[:, 288:295].astype(f32)
    source_quad = tail[:, 0]
    bias_quad = (tail[:, 1] + tail[:, 2] + tail[:, 3]).reshape(1536)
    square_quad = (tail[:, 4] + tail[:, 5] + tail[:, 6]).reshape(1536)
    x_quad = share(x_block, "z", 16)
    squares = jnp.pad(square_quad.reshape(12, 128), ((0, 4), (0, 0)))
    x_quad, dec_quad, squares = together((x_quad, dec_quad, squares))
    (partial,) = call(
        encode,
        x_quad,
        enc_quad,
        source_quad,
        squares,
        out=[((8, 400, 128), f32)],
        scratch=[pltpu.VMEM((16 * BLOCK, 128), f32), pltpu.VMEM((2, LAYERS, 288, 128), f32)],
    )
    partial = lax.all_to_all(partial, DP, 0, 0)
    pre, norms, acts, sparsity = call(
        activate,
        partial,
        bias_quad.reshape(12, 128),
        out=[((384, 128), f32), ((16, 128), f32), ((8, 384, 128), bf16), ((8, 128), f32)],
    )
    acts, x_sent = together((acts, x_quad))
    acts_quad = lax.all_to_all(acts, DP, 0, 0)

    (terms,) = call(decode, dec_quad, acts_quad, out=[((16, BLOCK, 128), bf16)])
    parts = lax.all_to_all(terms, "z", 0, 0)
    acts_every = lax.all_gather(acts_quad, QUAD)
    member = lax.axis_index(QUAD)
    acts_every = lax.dynamic_slice_in_dim(acts_every, member * 96, 96, 2)
    recon, gout = call(
        compare,
        parts,
        target_block,
        sparsity,
        out=[((BLOCK, 128), bf16), ((16, BLOCK, 128), bf16)],
    )
    x_every = lax.all_gather(x_sent.reshape(2, 8 * BLOCK, 128), QUAD)
    gout, x_every = together((gout, x_every))
    gout_all = lax.all_to_all(gout, "z", 0, 0)

    gout_every = lax.all_gather(gout_all.reshape(2, 8 * BLOCK, 128), QUAD)
    slopes, loss_z = call(
        pull_back, gout_all, dec_quad, out=[((8, 384, 128), bf16), ((8, 128), f32)]
    )
    slopes = lax.all_to_all(slopes, DP, 0, 0)
    recon = lax.ppermute(recon, ALL, back)
    slopes, recon = together((slopes, recon))
    (sent,) = call(slopes_of, slopes, pre, norms, loss_z, out=[((8, 112, 128), bf16)])
    got = lax.all_to_all(sent, PLANE, 0, 0)
    (sent,) = call(regroup, got, out=[((4, 784, 128), bf16)])
    got = lax.all_to_all(sent, "x", 0, 0)

    total = pltpu.VMEM((8 * BLOCK, 384), f32)
    own_norms = lax.dynamic_index_in_dim(norms[:12].reshape(4, 384), member, 0, True)
    (dec_grad,) = call(
        decoder_gradient,
        gout_every,
        acts_every,
        dec_t,
        own_norms,
        reach_wide,
        out=[((LAYERS, 288, 384), f32)],
        scratch=[total],
    )
    got, dec_grad = together((got, dec_grad))
    enc_grad, bias_grad, loss = call(
        encoder_gradient,
        x_every,
        got,
        pick.astype(f32),
        out=[((288, 384), f32), ((3, 128), f32), ((1, 1), f32)],
        scratch=[total],
    )
    recon = recon[:108].reshape(3, 36, 128).transpose(2, 0, 1)
    return (loss[0, 0], recon, enc_grad.T, bias_grad.reshape(384), dec_grad.transpose(2, 0, 1))


def solution(mesh):
    fine = Mesh(np.asarray(mesh.devices).reshape(SIZES), ALL)
    in_specs = (
        P(DP, None, LATENT),
        P(DP, None, LATENT),
        P(LATENT, DP),
        P(LATENT),
        P(LATENT, None, DP),
        P(LATENT),
    )
    out_specs = (
        P(),
        P(DP, None, LATENT),
        P(LATENT, DP),
        P(LATENT),
        P(LATENT, None, DP),
    )
    return jax.shard_map(
        on_device, mesh=fine, in_specs=in_specs, out_specs=out_specs, check_vma=False
    )
```

```python
import jax
import jax.numpy as jnp
import numpy as np
from jax import lax
from jax.experimental import pallas as pl
from jax.experimental.pallas import tpu as pltpu
from jax.sharding import Mesh
from jax.sharding import PartitionSpec as P

LAYERS = 3
TOK_DEV = 128
SIZES = (4, 2, 16, 2, 2)
ALL = ("x", "yh", "z", "yl", "c")
DP = ("x", "yh")
LATENT = ("z", "yl", "c")
QUAD = ("yl", "c")
PLANE = ("yh", "yl", "c")
BLOCK = 112

sparsity_weight = 0.5
norm_epsilon = 1e-06
bf16, f32 = jnp.bfloat16, jnp.float32


def spread():
    pairs = []
    for a in range(8):
        for b in range(64):
            i, r = divmod(b, 8)
            pairs.append((a * 64 + b, i * 64 + ((a % 2) * 8 + r) * 4 + a // 2))
    return pairs


def pieces(value):
    high = lax.reduce_precision(value, 8, 7)
    middle = lax.reduce_precision(value - high, 8, 7)
    low = value - high - middle
    return [high.astype(bf16), middle.astype(bf16), low.astype(bf16)]


def share(block, axes, count):
    return lax.all_to_all(jnp.broadcast_to(block[None], (count, *block.shape)), axes, 0, 0)


def call(kernel, *args, out, scratch=()):
    return pl.pallas_call(
        kernel,
        out_shape=[jax.ShapeDtypeStruct(shape, dtype) for shape, dtype in out],
        scratch_shapes=scratch,
        compiler_params=pltpu.CompilerParams(vmem_limit_bytes=40 * 1024 * 1024),
    )(*args)


def split(value):
    high = value.astype(bf16)
    rest = value - high.astype(f32)
    middle = rest.astype(bf16)
    return [high, middle, (rest - middle.astype(f32)).astype(bf16)]


def matmul(a, b, left, right):
    return lax.dot_general(a, b, (((left,), (right,)), ((), ())), preferred_element_type=f32)


def spread_out(both, out):
    for z in range(16):
        out[z] = both[0]


def arrange(dec, source, out, square, masked, ordered):
    total = jnp.zeros((1, 384), f32)
    for layer in range(LAYERS):
        masked[...] = jnp.where(source[...] <= layer, dec[layer].astype(f32), 0.0)
        total = total + jnp.sum(masked[...] * masked[...], axis=0, keepdims=True)
        for r in range(8):
            at = r * BLOCK + layer * 36
            ordered[at : at + 36] = masked[r * 36 : r * 36 + 36]
    for r in range(8):
        ordered[r * BLOCK + 108 : (r + 1) * BLOCK] = jnp.zeros((BLOCK - 108, 384), f32)
    out[...] = ordered[...].astype(bf16)
    square[...] = total


def encode(x, rows, sources, bias, squares, out, wide, by_layer):
    wide[...] = x[...].reshape(16 * BLOCK, 128).astype(f32)
    for half in range(2):
        for layer in range(LAYERS):
            for r in range(8):
                at = (half * 8 + r) * BLOCK + layer * 36
                by_layer[half, layer, r * 36 : r * 36 + 36] = wide[at : at + 36]
    for half in range(2):
        tokens = [by_layer[half, layer].astype(bf16) for layer in range(LAYERS)]
        for q in range(4):
            product = jnp.broadcast_to(bias[q : q + 1] * 0.125, (128, 384))
            for layer in range(LAYERS):
                here = matmul(tokens[layer], rows[q, 0:288], 0, 0)
                product = product + jnp.where(sources[q : q + 1] == layer, here, 0.0)
            for g in range(4):
                for c in range(3):
                    at = (q * 3 + c) * 32
                    out[half * 4 + g, at : at + 32] = product[
                        g * 32 : g * 32 + 32, c * 128 : c * 128 + 128
                    ]
    for g in range(8):
        out[g, 384:] = squares[...]


def activate(parts, state, acts):
    total = jnp.sum(parts[...], axis=0)
    norm = jnp.sqrt(total[384:396] + norm_epsilon)
    state[0:384] = total[0:384]
    state[384:396] = norm
    state[396:400] = jnp.zeros((4, 128), f32)
    weighted = jnp.zeros((32, 128), f32)
    for c in range(12):
        low = jnp.maximum(total[c * 32 : c * 32 + 32], 0.0).astype(bf16)
        weighted = weighted + low.astype(f32) * norm[c : c + 1]
        for g in range(8):
            acts[g, c * 32 : c * 32 + 32] = low
    state[400:408] = jnp.broadcast_to(jnp.sum(weighted, axis=0, keepdims=True), (8, 128))


def tokens_of(ref, half, column):
    return ref[half * 4 : half * 4 + 4, column * 32 : column * 32 + 32].reshape(128, 128)


def decode(rows, acts, out):
    for half in range(2):
        total = None
        for q in range(4):
            wide = jnp.concatenate([tokens_of(acts, half, q * 3 + c) for c in range(3)], axis=1)
            product = matmul(rows[q], wide, 1, 1)
            total = product if total is None else total + product
        low = total.astype(bf16)
        for r in range(8):
            out[half * 8 + r] = low[r * BLOCK : (r + 1) * BLOCK]


def compare(parts, both, state, recon, gout):
    recon_sum = jnp.sum(parts[...].astype(f32), axis=0)
    recon[...] = recon_sum.astype(bf16)
    error = recon_sum - both[1].astype(f32)
    by_lane = jnp.sum(error * error, axis=0, keepdims=True) + sparsity_weight * state[400:401]
    slope = 2.0 * error / TOK_DEV
    row = lax.broadcasted_iota(jnp.int32, (BLOCK, 128), 0)
    for k, piece in enumerate(split(by_lane)):
        slope = jnp.where(row == 108 + k, piece.astype(f32), slope)
    low = slope.astype(bf16)
    for z in range(16):
        gout[z] = low


def pull_back(gout, rows, out, loss):
    total = jnp.sum(gout[:, 96:112].astype(f32), axis=0)
    loss[...] = jnp.broadcast_to(jnp.sum(total[12:15], axis=0, keepdims=True), (8, 128))
    for half in range(2):
        tokens = jnp.concatenate([gout[half * 8 + r] for r in range(8)], axis=0)
        for q in range(4):
            product = matmul(tokens, rows[q], 0, 0).astype(bf16)
            for g in range(4):
                for c in range(3):
                    at = (q * 3 + c) * 32
                    out[half * 4 + g, at : at + 32] = product[
                        g * 32 : g * 32 + 32, c * 128 : c * 128 + 128
                    ]


def tail_of(values):
    row = lax.broadcasted_iota(jnp.int32, (16, 128), 0)
    tail = jnp.zeros((16, 128), f32)
    for k, value in enumerate(values):
        for p, piece in enumerate(split(value)):
            tail = jnp.where(row == 4 * p + k, piece.astype(f32), tail)
    return tail.astype(bf16)


def slopes_of(parts, state, loss, out):
    total = jnp.sum(parts[...].astype(f32), axis=0)
    for q in range(4):
        sums = []
        for c in range(3):
            k = q * 3 + c
            norm = state[384 + k : 385 + k]
            slope = total[k * 32 : k * 32 + 32] + (sparsity_weight / TOK_DEV) * norm
            slope = jnp.where(state[k * 32 : k * 32 + 32] > 0, slope, 0.0)
            sums.append(jnp.sum(slope, axis=0, keepdims=True))
            for yh in range(2):
                out[yh * 4 + q, c * 32 : c * 32 + 32] = slope.astype(bf16)
        tail = tail_of([*sums, loss[0:1]])
        for yh in range(2):
            out[yh * 4 + q, 96:112] = tail


def regroup(got, out):
    tail = jnp.sum(got[:, 96:112].astype(f32), axis=0)
    tail = tail[0:4] + tail[4:8] + tail[8:12]
    tail = tail_of([tail[k : k + 1] for k in range(4)])
    for x in range(4):
        for m in range(8):
            out[x, m * 96 : m * 96 + 96] = got[m, 0:96]
        out[x, 768:784] = tail


def over_tokens(blocks, values):
    total = None
    for q in range(4):
        wide = jnp.concatenate([blocks[q, 0], blocks[q, 1]], axis=1)
        column = lambda c: jnp.concatenate([values(h, q, c) for h in range(2)], axis=0)
        product = matmul(wide, jnp.concatenate([column(c) for c in range(3)], axis=1), 1, 0)
        total = product if total is None else total + product
    return total


def decoder_gradient(blocks, acts, rows, norms, source, out, total):
    def values(half, q, c):
        here = acts[q, half * 4 : half * 4 + 4, c * 32 : c * 32 + 32]
        return here.reshape(128, 128)

    total[...] = over_tokens(blocks, values)
    sums = []
    for c in range(3):
        column = acts[:, :, c * 32 : c * 32 + 32].reshape(1024, 128).astype(f32)
        sums.append(jnp.sum(column, axis=0, keepdims=True))
    pull = (sparsity_weight / TOK_DEV) * jnp.concatenate(sums, axis=1) / norms[...]
    for layer in range(LAYERS):
        for r in range(8):
            at = r * BLOCK + layer * 36
            out[layer, r * 36 : r * 36 + 36] = total[at : at + 36]
        whole = out[layer] + pull * rows[layer].astype(f32)
        out[layer] = jnp.where(source[...] <= layer, whole, 0.0)


def encoder_gradient(blocks, dpre, source, out, bias, loss, total):
    def values(half, q, c):
        parts = [
            dpre[half * 2 + g // 2, pl.ds(((g % 2) * 4 + q) * 96 + c * 32, 32)] for g in range(4)
        ]
        return jnp.concatenate(parts, axis=0)

    total[...] = over_tokens(blocks, values)
    for r in range(8):
        own = jnp.zeros((36, 384), f32)
        for layer in range(LAYERS):
            at = r * BLOCK + layer * 36
            own = own + jnp.where(source[...] == layer, total[at : at + 36], 0.0)
        out[r * 36 : r * 36 + 36] = own
    tail = jnp.sum(dpre[:, 768:784].astype(f32), axis=0)
    tail = tail[0:4] + tail[4:8] + tail[8:12]
    bias[...] = tail[0:3]
    loss[...] = jnp.sum(tail[3:4], axis=1, keepdims=True) / TOK_DEV


together = lax.optimization_barrier


def on_device(resid, target, enc_weight, enc_bias, dec_weight, source):
    to = spread()
    back = [(d, s) for s, d in to]
    source_row = source[None]

    both = jnp.stack([resid, target]).transpose(0, 2, 3, 1).reshape(2, 108, 128)
    both = jnp.pad(both, ((0, 0), (0, BLOCK - 108), (0, 0)))
    both = lax.ppermute(both, ALL, to)

    enc_t = enc_weight.T
    dec_t = dec_weight.transpose(1, 2, 0)
    dec_own, square = call(
        arrange,
        dec_t,
        source_row,
        out=[((8 * BLOCK, 384), bf16), ((1, 384), f32)],
        scratch=[pltpu.VMEM((288, 384), f32), pltpu.VMEM((8 * BLOCK, 384), f32)],
    )
    extra = jnp.stack([source.astype(bf16), *pieces(enc_bias), *pieces(square[0])])
    enc_own = jnp.concatenate([enc_t, jnp.pad(extra, ((0, 9), (0, 0)))])
    enc_quad = lax.all_gather(enc_own, QUAD)
    dec_quad = lax.all_gather(dec_own, QUAD)
    tail = enc_quad[:, 288:295].astype(f32)
    source_quad = tail[:, 0]
    bias_quad = tail[:, 1] + tail[:, 2] + tail[:, 3]
    square_quad = (tail[:, 4] + tail[:, 5] + tail[:, 6]).reshape(1536)
    (x_sent,) = call(spread_out, both, out=[((16, BLOCK, 128), bf16)])
    x_quad = lax.all_to_all(x_sent, "z", 0, 0)
    squares = jnp.pad(square_quad.reshape(12, 128), ((0, 4), (0, 0)))
    x_quad, dec_quad, squares = together((x_quad, dec_quad, squares))
    (partial,) = call(
        encode,
        x_quad,
        enc_quad,
        source_quad,
        bias_quad,
        squares,
        out=[((8, 400, 128), f32)],
        scratch=[pltpu.VMEM((16 * BLOCK, 128), f32), pltpu.VMEM((2, LAYERS, 288, 128), f32)],
    )
    partial = lax.all_to_all(partial, DP, 0, 0)
    state, acts = call(
        activate, partial, out=[((408, 128), f32), ((8, 384, 128), bf16)]
    )
    acts, x_sent = together((acts, x_quad))
    acts_quad = lax.all_to_all(acts, DP, 0, 0)

    (terms,) = call(decode, dec_quad, acts_quad, out=[((16, BLOCK, 128), bf16)])
    parts = lax.all_to_all(terms, "z", 0, 0)
    acts_every = lax.all_gather(acts_quad, QUAD)
    member = lax.axis_index(QUAD)
    acts_every = lax.dynamic_slice_in_dim(acts_every, member * 96, 96, 2)
    recon, gout = call(
        compare,
        parts,
        both,
        state,
        out=[((BLOCK, 128), bf16), ((16, BLOCK, 128), bf16)],
    )
    x_every = lax.all_gather(x_sent.reshape(2, 8 * BLOCK, 128), QUAD)
    gout, x_every = together((gout, x_every))
    gout_all = lax.all_to_all(gout, "z", 0, 0)

    gout_every = lax.all_gather(gout_all.reshape(2, 8 * BLOCK, 128), QUAD)
    slopes, loss_z = call(
        pull_back, gout_all, dec_quad, out=[((8, 384, 128), bf16), ((8, 128), f32)]
    )
    slopes = lax.all_to_all(slopes, DP, 0, 0)
    (sent,) = call(slopes_of, slopes, state, loss_z, out=[((8, 112, 128), bf16)])
    got = lax.all_to_all(sent, PLANE, 0, 0)
    (sent,) = call(regroup, got, out=[((4, 784, 128), bf16)])
    got = lax.all_to_all(sent, "x", 0, 0)

    total = pltpu.VMEM((8 * BLOCK, 384), f32)
    own_norms = lax.dynamic_index_in_dim(state[384:396].reshape(4, 384), member, 0, True)
    (dec_grad,) = call(
        decoder_gradient,
        gout_every,
        acts_every,
        dec_t,
        own_norms,
        source_row,
        out=[((LAYERS, 288, 384), f32)],
        scratch=[total],
    )
    got, dec_grad = together((got, dec_grad))
    enc_grad, bias_grad, loss = call(
        encoder_gradient,
        x_every,
        got,
        source_row,
        out=[((288, 384), f32), ((3, 128), f32), ((1, 1), f32)],
        scratch=[total],
    )
    recon = lax.ppermute(recon, ALL, back)
    recon, enc_grad = together((recon, enc_grad))
    recon = recon[:108].reshape(3, 36, 128).transpose(2, 0, 1)
    return (loss[0, 0], recon, enc_grad.T, bias_grad.reshape(384), dec_grad.transpose(2, 0, 1))


def solution(mesh):
    fine = Mesh(np.asarray(mesh.devices).reshape(SIZES), ALL)
    in_specs = (
        P(DP, None, LATENT),
        P(DP, None, LATENT),
        P(LATENT, DP),
        P(LATENT),
        P(LATENT, None, DP),
        P(LATENT),
    )
    out_specs = (
        P(),
        P(DP, None, LATENT),
        P(LATENT, DP),
        P(LATENT),
        P(LATENT, None, DP),
    )
    return jax.shard_map(
        on_device, mesh=fine, in_specs=in_specs, out_specs=out_specs, check_vma=False
    )
```

```python
import jax
import jax.numpy as jnp
import numpy as np
from jax import lax
from jax.experimental import pallas as pl
from jax.experimental.pallas import tpu as pltpu
from jax.sharding import Mesh
from jax.sharding import PartitionSpec as P

LAYERS = 3
TOK_DEV = 128
SIZES = (4, 2, 16, 2, 2)
ALL = ("x", "yh", "z", "yl", "c")
DP = ("x", "yh")
LATENT = ("z", "yl", "c")
QUAD = ("yl", "c")
PLANE = ("yh", "yl", "c")
BLOCK = 112

sparsity_weight = 0.5
norm_epsilon = 1e-06
bf16, f32 = jnp.bfloat16, jnp.float32


def spread():
    pairs = []
    for a in range(8):
        for b in range(64):
            i, r = divmod(b, 8)
            pairs.append((a * 64 + b, i * 64 + ((a % 2) * 8 + r) * 4 + a // 2))
    return pairs


def pieces(value):
    high = lax.reduce_precision(value, 8, 7)
    middle = lax.reduce_precision(value - high, 8, 7)
    low = value - high - middle
    return [high.astype(bf16), middle.astype(bf16), low.astype(bf16)]


def share(block, axes, count):
    return lax.all_to_all(jnp.broadcast_to(block[None], (count, *block.shape)), axes, 0, 0)


def call(kernel, *args, out, far=(), scratch=()):
    inside = pl.BlockSpec(memory_space=pltpu.VMEM)
    outside = pl.BlockSpec(memory_space=pltpu.HBM)
    shapes = [
        pltpu.HBM(shape, dtype) if k in far else jax.ShapeDtypeStruct(shape, dtype)
        for k, (shape, dtype) in enumerate(out)
    ]
    return pl.pallas_call(
        kernel,
        in_specs=[inside] * len(args),
        out_specs=[outside if k in far else inside for k in range(len(out))],
        out_shape=shapes,
        scratch_shapes=scratch,
        compiler_params=pltpu.CompilerParams(vmem_limit_bytes=40 * 1024 * 1024),
    )(*args)


def split(value):
    high = value.astype(bf16)
    rest = value - high.astype(f32)
    middle = rest.astype(bf16)
    return [high, middle, (rest - middle.astype(f32)).astype(bf16)]


def matmul(a, b, left, right):
    return lax.dot_general(a, b, (((left,), (right,)), ((), ())), preferred_element_type=f32)


def spread_out(both, out):
    for z in range(16):
        out[z] = both[0]


def arrange(dec, source, out, square, masked, ordered):
    total = jnp.zeros((1, 384), f32)
    for layer in range(LAYERS):
        masked[...] = jnp.where(source[...] <= layer, dec[layer].astype(f32), 0.0)
        total = total + jnp.sum(masked[...] * masked[...], axis=0, keepdims=True)
        for r in range(8):
            at = r * BLOCK + layer * 36
            ordered[at : at + 36] = masked[r * 36 : r * 36 + 36]
    for r in range(8):
        ordered[r * BLOCK + 108 : (r + 1) * BLOCK] = jnp.zeros((BLOCK - 108, 384), f32)
    out[...] = ordered[...].astype(bf16)
    square[...] = total


def encode(x, rows, sources, bias, squares, out, kept, wide, by_layer, sem):
    copy = pltpu.make_async_copy(x, kept, sem)
    copy.start()
    wide[...] = x[...].reshape(16 * BLOCK, 128).astype(f32)
    for half in range(2):
        for layer in range(LAYERS):
            for r in range(8):
                at = (half * 8 + r) * BLOCK + layer * 36
                by_layer[half, layer, r * 36 : r * 36 + 36] = wide[at : at + 36]
    for half in range(2):
        tokens = [by_layer[half, layer].astype(bf16) for layer in range(LAYERS)]
        for q in range(4):
            product = jnp.broadcast_to(bias[q : q + 1] * 0.125, (128, 384))
            for layer in range(LAYERS):
                here = matmul(tokens[layer], rows[q, 0:288], 0, 0)
                product = product + jnp.where(sources[q : q + 1] == layer, here, 0.0)
            for g in range(4):
                for c in range(3):
                    at = (q * 3 + c) * 32
                    out[half * 4 + g, at : at + 32] = product[
                        g * 32 : g * 32 + 32, c * 128 : c * 128 + 128
                    ]
    for g in range(8):
        out[g, 384:] = squares[...]
    copy.wait()


def activate(parts, far_state, acts, state, sem):
    total = jnp.sum(parts[...], axis=0)
    norm = jnp.sqrt(total[384:396] + norm_epsilon)
    state[0:384] = total[0:384]
    state[384:396] = norm
    state[396:400] = jnp.zeros((4, 128), f32)
    lows = [jnp.maximum(total[c * 32 : c * 32 + 32], 0.0).astype(bf16) for c in range(12)]
    weighted = jnp.zeros((32, 128), f32)
    for c in range(12):
        weighted = weighted + lows[c].astype(f32) * norm[c : c + 1]
    state[400:408] = jnp.broadcast_to(jnp.sum(weighted, axis=0, keepdims=True), (8, 128))
    copy = pltpu.make_async_copy(state, far_state, sem)
    copy.start()
    for c in range(12):
        for g in range(8):
            acts[g, c * 32 : c * 32 + 32] = lows[c]
    copy.wait()


def tokens_of(ref, half, column):
    return ref[half * 4 : half * 4 + 4, column * 32 : column * 32 + 32].reshape(128, 128)


def decode(rows, acts, out, kept, sem):
    copy = pltpu.make_async_copy(acts, kept, sem)
    copy.start()
    for half in range(2):
        total = None
        for q in range(4):
            wide = jnp.concatenate([tokens_of(acts, half, q * 3 + c) for c in range(3)], axis=1)
            product = matmul(rows[q], wide, 1, 1)
            total = product if total is None else total + product
        low = total.astype(bf16)
        for r in range(8):
            out[half * 8 + r] = low[r * BLOCK : (r + 1) * BLOCK]
    copy.wait()


def compare(parts, both, state, recon, gout):
    recon_sum = jnp.sum(parts[...].astype(f32), axis=0)
    recon[...] = recon_sum.astype(bf16)
    error = recon_sum - both[1].astype(f32)
    by_lane = jnp.sum(error * error, axis=0, keepdims=True) + sparsity_weight * state[400:401]
    slope = 2.0 * error / TOK_DEV
    row = lax.broadcasted_iota(jnp.int32, (BLOCK, 128), 0)
    for k, piece in enumerate(split(by_lane)):
        slope = jnp.where(row == 108 + k, piece.astype(f32), slope)
    low = slope.astype(bf16)
    for z in range(16):
        gout[z] = low


def pull_back(gout, rows, out, loss, kept, sem):
    copy = pltpu.make_async_copy(gout, kept, sem)
    copy.start()
    total = jnp.sum(gout[:, 96:112].astype(f32), axis=0)
    loss[...] = jnp.broadcast_to(jnp.sum(total[12:15], axis=0, keepdims=True), (8, 128))
    for half in range(2):
        tokens = jnp.concatenate([gout[half * 8 + r] for r in range(8)], axis=0)
        for q in range(4):
            product = matmul(tokens, rows[q], 0, 0).astype(bf16)
            for g in range(4):
                for c in range(3):
                    at = (q * 3 + c) * 32
                    out[half * 4 + g, at : at + 32] = product[
                        g * 32 : g * 32 + 32, c * 128 : c * 128 + 128
                    ]
    copy.wait()


def tail_of(values):
    row = lax.broadcasted_iota(jnp.int32, (16, 128), 0)
    tail = jnp.zeros((16, 128), f32)
    for k, value in enumerate(values):
        for p, piece in enumerate(split(value)):
            tail = jnp.where(row == 4 * p + k, piece.astype(f32), tail)
    return tail.astype(bf16)


def slopes_of(parts, state, loss, out):
    total = jnp.sum(parts[...].astype(f32), axis=0)
    for q in range(4):
        sums = []
        for c in range(3):
            k = q * 3 + c
            norm = state[384 + k : 385 + k]
            slope = total[k * 32 : k * 32 + 32] + (sparsity_weight / TOK_DEV) * norm
            slope = jnp.where(state[k * 32 : k * 32 + 32] > 0, slope, 0.0)
            sums.append(jnp.sum(slope, axis=0, keepdims=True))
            for yh in range(2):
                out[yh * 4 + q, c * 32 : c * 32 + 32] = slope.astype(bf16)
        tail = tail_of([*sums, loss[0:1]])
        for yh in range(2):
            out[yh * 4 + q, 96:112] = tail


def regroup(got, out):
    tail = jnp.sum(got[:, 96:112].astype(f32), axis=0)
    tail = tail[0:4] + tail[4:8] + tail[8:12]
    tail = tail_of([tail[k : k + 1] for k in range(4)])
    for x in range(4):
        for m in range(8):
            out[x, m * 96 : m * 96 + 96] = got[m, 0:96]
        out[x, 768:784] = tail


def over_tokens(blocks, values):
    total = None
    for q in range(4):
        wide = jnp.concatenate([blocks[q, 0], blocks[q, 1]], axis=1)
        column = lambda c: jnp.concatenate([values(h, q, c) for h in range(2)], axis=0)
        product = matmul(wide, jnp.concatenate([column(c) for c in range(3)], axis=1), 1, 0)
        total = product if total is None else total + product
    return total


def decoder_gradient(blocks, acts, rows, norms, source, out, total):
    def values(half, q, c):
        here = acts[q, half * 4 : half * 4 + 4, c * 32 : c * 32 + 32]
        return here.reshape(128, 128)

    total[...] = over_tokens(blocks, values)
    sums = []
    for c in range(3):
        column = acts[:, :, c * 32 : c * 32 + 32].reshape(1024, 128).astype(f32)
        sums.append(jnp.sum(column, axis=0, keepdims=True))
    pull = (sparsity_weight / TOK_DEV) * jnp.concatenate(sums, axis=1) / norms[...]
    for layer in range(LAYERS):
        for r in range(8):
            at = r * BLOCK + layer * 36
            out[layer, r * 36 : r * 36 + 36] = total[at : at + 36]
        whole = out[layer] + pull * rows[layer].astype(f32)
        out[layer] = jnp.where(source[...] <= layer, whole, 0.0)


def encoder_gradient(blocks, dpre, source, out, bias, loss, total):
    def values(half, q, c):
        parts = [
            dpre[half * 2 + g // 2, pl.ds(((g % 2) * 4 + q) * 96 + c * 32, 32)] for g in range(4)
        ]
        return jnp.concatenate(parts, axis=0)

    total[...] = over_tokens(blocks, values)
    for r in range(8):
        own = jnp.zeros((36, 384), f32)
        for layer in range(LAYERS):
            at = r * BLOCK + layer * 36
            own = own + jnp.where(source[...] == layer, total[at : at + 36], 0.0)
        out[r * 36 : r * 36 + 36] = own
    tail = jnp.sum(dpre[:, 768:784].astype(f32), axis=0)
    tail = tail[0:4] + tail[4:8] + tail[8:12]
    bias[...] = tail[0:3]
    loss[...] = jnp.sum(tail[3:4], axis=1, keepdims=True) / TOK_DEV


together = lax.optimization_barrier


def on_device(resid, target, enc_weight, enc_bias, dec_weight, source):
    to = spread()
    back = [(d, s) for s, d in to]
    source_row = source[None]

    both = jnp.stack([resid, target]).transpose(0, 2, 3, 1).reshape(2, 108, 128)
    both = jnp.pad(both, ((0, 0), (0, BLOCK - 108), (0, 0)))
    both = lax.ppermute(both, ALL, to)

    enc_t = enc_weight.T
    dec_t = dec_weight.transpose(1, 2, 0)
    dec_own, square = call(
        arrange,
        dec_t,
        source_row,
        out=[((8 * BLOCK, 384), bf16), ((1, 384), f32)],
        scratch=[pltpu.VMEM((288, 384), f32), pltpu.VMEM((8 * BLOCK, 384), f32)],
    )
    extra = jnp.stack([source.astype(bf16), *pieces(enc_bias), *pieces(square[0])])
    enc_own = jnp.concatenate([enc_t, jnp.pad(extra, ((0, 9), (0, 0)))])
    enc_quad = lax.all_gather(enc_own, QUAD)
    dec_quad = lax.all_gather(dec_own, QUAD)
    tail = enc_quad[:, 288:295].astype(f32)
    source_quad = tail[:, 0]
    bias_quad = tail[:, 1] + tail[:, 2] + tail[:, 3]
    square_quad = (tail[:, 4] + tail[:, 5] + tail[:, 6]).reshape(1536)
    (x_sent,) = call(spread_out, both, out=[((16, BLOCK, 128), bf16)])
    x_quad = lax.all_to_all(x_sent, "z", 0, 0)
    squares = jnp.pad(square_quad.reshape(12, 128), ((0, 4), (0, 0)))
    x_quad, dec_quad, squares = together((x_quad, dec_quad, squares))
    partial, x_kept = call(
        encode,
        x_quad,
        enc_quad,
        source_quad,
        bias_quad,
        squares,
        out=[((8, 400, 128), f32), ((16, BLOCK, 128), bf16)],
        far=(1,),
        scratch=[
            pltpu.VMEM((16 * BLOCK, 128), f32),
            pltpu.VMEM((2, LAYERS, 288, 128), f32),
            pltpu.SemaphoreType.DMA,
        ],
    )
    partial = lax.all_to_all(partial, DP, 0, 0)
    state, acts = call(
        activate,
        partial,
        out=[((408, 128), f32), ((8, 384, 128), bf16)],
        far=(0,),
        scratch=[pltpu.VMEM((408, 128), f32), pltpu.SemaphoreType.DMA],
    )
    acts, x_sent = together((acts, x_kept))
    acts_quad = lax.all_to_all(acts, DP, 0, 0)

    terms, acts_kept = call(
        decode,
        dec_quad,
        acts_quad,
        out=[((16, BLOCK, 128), bf16), ((8, 384, 128), bf16)],
        far=(1,),
        scratch=[pltpu.SemaphoreType.DMA],
    )
    parts = lax.all_to_all(terms, "z", 0, 0)
    acts_every = lax.all_gather(acts_kept, QUAD)
    member = lax.axis_index(QUAD)
    acts_every = lax.dynamic_slice_in_dim(acts_every, member * 96, 96, 2)
    recon, gout = call(
        compare,
        parts,
        both,
        state,
        out=[((BLOCK, 128), bf16), ((16, BLOCK, 128), bf16)],
    )
    x_every = lax.all_gather(x_sent.reshape(2, 8 * BLOCK, 128), QUAD)
    gout, x_every = together((gout, x_every))
    gout_all = lax.all_to_all(gout, "z", 0, 0)

    slopes, loss_z, gout_kept = call(
        pull_back,
        gout_all,
        dec_quad,
        out=[((8, 384, 128), bf16), ((8, 128), f32), ((16, BLOCK, 128), bf16)],
        far=(2,),
        scratch=[pltpu.SemaphoreType.DMA],
    )
    gout_every = lax.all_gather(gout_kept.reshape(2, 8 * BLOCK, 128), QUAD)
    slopes = lax.all_to_all(slopes, DP, 0, 0)
    (sent,) = call(slopes_of, slopes, state, loss_z, out=[((8, 112, 128), bf16)])
    got = lax.all_to_all(sent, PLANE, 0, 0)
    (sent,) = call(regroup, got, out=[((4, 784, 128), bf16)])
    got = lax.all_to_all(sent, "x", 0, 0)

    total = pltpu.VMEM((8 * BLOCK, 384), f32)
    own_norms = lax.dynamic_index_in_dim(state[384:396].reshape(4, 384), member, 0, True)
    (dec_grad,) = call(
        decoder_gradient,
        gout_every,
        acts_every,
        dec_t,
        own_norms,
        source_row,
        out=[((LAYERS, 288, 384), f32)],
        scratch=[total],
    )
    got, dec_grad = together((got, dec_grad))
    enc_grad, bias_grad, loss = call(
        encoder_gradient,
        x_every,
        got,
        source_row,
        out=[((288, 384), f32), ((3, 128), f32), ((1, 1), f32)],
        scratch=[total],
    )
    recon = lax.ppermute(recon, ALL, back)
    recon, enc_grad = together((recon, enc_grad))
    recon = recon[:108].reshape(3, 36, 128).transpose(2, 0, 1)
    return (loss[0, 0], recon, enc_grad.T, bias_grad.reshape(384), dec_grad.transpose(2, 0, 1))


def solution(mesh):
    fine = Mesh(np.asarray(mesh.devices).reshape(SIZES), ALL)
    in_specs = (
        P(DP, None, LATENT),
        P(DP, None, LATENT),
        P(LATENT, DP),
        P(LATENT),
        P(LATENT, None, DP),
        P(LATENT),
    )
    out_specs = (
        P(),
        P(DP, None, LATENT),
        P(LATENT, DP),
        P(LATENT),
        P(LATENT, None, DP),
    )
    return jax.shard_map(
        on_device, mesh=fine, in_specs=in_specs, out_specs=out_specs, check_vma=False
    )
```

```python
import jax
import jax.numpy as jnp
import numpy as np
from jax import lax
from jax.experimental import pallas as pl
from jax.experimental.pallas import tpu as pltpu
from jax.sharding import Mesh
from jax.sharding import PartitionSpec as P

LAYERS = 3
TOK_DEV = 128
SIZES = (4, 2, 16, 2, 2)
ALL = ("x", "yh", "z", "yl", "c")
DP = ("x", "yh")
LATENT = ("z", "yl", "c")
QUAD = ("yl", "c")
PLANE = ("yh", "yl", "c")
BLOCK = 112

sparsity_weight = 0.5
norm_epsilon = 1e-06
bf16, f32 = jnp.bfloat16, jnp.float32


def spread():
    pairs = []
    for a in range(8):
        for b in range(64):
            i, r = divmod(b, 8)
            pairs.append((a * 64 + b, i * 64 + ((a % 2) * 8 + r) * 4 + a // 2))
    return pairs


def pieces(value):
    high = lax.reduce_precision(value, 8, 7)
    middle = lax.reduce_precision(value - high, 8, 7)
    low = value - high - middle
    return [high.astype(bf16), middle.astype(bf16), low.astype(bf16)]


def share(block, axes, count):
    return lax.all_to_all(jnp.broadcast_to(block[None], (count, *block.shape)), axes, 0, 0)


def call(kernel, *args, out, far=(), scratch=()):
    inside = pl.BlockSpec(memory_space=pltpu.VMEM)
    outside = pl.BlockSpec(memory_space=pltpu.HBM)
    shapes = [
        pltpu.HBM(shape, dtype) if k in far else jax.ShapeDtypeStruct(shape, dtype)
        for k, (shape, dtype) in enumerate(out)
    ]
    return pl.pallas_call(
        kernel,
        in_specs=[inside] * len(args),
        out_specs=[outside if k in far else inside for k in range(len(out))],
        out_shape=shapes,
        scratch_shapes=scratch,
        compiler_params=pltpu.CompilerParams(vmem_limit_bytes=40 * 1024 * 1024),
    )(*args)


def split(value):
    high = value.astype(bf16)
    rest = value - high.astype(f32)
    middle = rest.astype(bf16)
    return [high, middle, (rest - middle.astype(f32)).astype(bf16)]


def matmul(a, b, left, right):
    return lax.dot_general(a, b, (((left,), (right,)), ((), ())), preferred_element_type=f32)


def spread_out(both, out, kept, sem):
    copy = pltpu.make_async_copy(both, kept, sem)
    copy.start()
    for z in range(16):
        out[z] = both[0]
    copy.wait()


def arrange(dec, source, out, square, masked, ordered):
    total = jnp.zeros((1, 384), f32)
    for layer in range(LAYERS):
        masked[...] = jnp.where(source[...] <= layer, dec[layer].astype(f32), 0.0)
        total = total + jnp.sum(masked[...] * masked[...], axis=0, keepdims=True)
        for r in range(8):
            at = r * BLOCK + layer * 36
            ordered[at : at + 36] = masked[r * 36 : r * 36 + 36]
    for r in range(8):
        ordered[r * BLOCK + 108 : (r + 1) * BLOCK] = jnp.zeros((BLOCK - 108, 384), f32)
    out[...] = ordered[...].astype(bf16)
    square[...] = total


def encode(x, rows, sources, bias, squares, out, kept, wide, by_layer, sem):
    copy = pltpu.make_async_copy(x, kept, sem)
    copy.start()
    wide[...] = x[...].reshape(16 * BLOCK, 128).astype(f32)
    for half in range(2):
        for layer in range(LAYERS):
            for r in range(8):
                at = (half * 8 + r) * BLOCK + layer * 36
                by_layer[half, layer, r * 36 : r * 36 + 36] = wide[at : at + 36]
    for half in range(2):
        tokens = [by_layer[half, layer].astype(bf16) for layer in range(LAYERS)]
        for q in range(4):
            product = jnp.broadcast_to(bias[q : q + 1] * 0.125, (128, 384))
            for layer in range(LAYERS):
                here = matmul(tokens[layer], rows[q, 0:288], 0, 0)
                product = product + jnp.where(sources[q : q + 1] == layer, here, 0.0)
            for g in range(4):
                for c in range(3):
                    at = (q * 3 + c) * 32
                    out[half * 4 + g, at : at + 32] = product[
                        g * 32 : g * 32 + 32, c * 128 : c * 128 + 128
                    ]
    for g in range(8):
        out[g, 384:] = squares[...]
    copy.wait()


def activate(parts, far_state, acts, state, sem):
    total = jnp.sum(parts[...], axis=0)
    norm = jnp.sqrt(total[384:396] + norm_epsilon)
    state[0:384] = total[0:384]
    state[384:396] = norm
    state[396:400] = jnp.zeros((4, 128), f32)
    lows = [jnp.maximum(total[c * 32 : c * 32 + 32], 0.0).astype(bf16) for c in range(12)]
    weighted = jnp.zeros((32, 128), f32)
    for c in range(12):
        weighted = weighted + lows[c].astype(f32) * norm[c : c + 1]
    state[400:408] = jnp.broadcast_to(jnp.sum(weighted, axis=0, keepdims=True), (8, 128))
    copy = pltpu.make_async_copy(state, far_state, sem)
    copy.start()
    for c in range(12):
        for g in range(8):
            acts[g, c * 32 : c * 32 + 32] = lows[c]
    copy.wait()


def tokens_of(ref, half, column):
    return ref[half * 4 : half * 4 + 4, column * 32 : column * 32 + 32].reshape(128, 128)


def decode(rows, acts, out, kept, sem):
    copy = pltpu.make_async_copy(acts, kept, sem)
    copy.start()
    for half in range(2):
        total = None
        for q in range(4):
            wide = jnp.concatenate([tokens_of(acts, half, q * 3 + c) for c in range(3)], axis=1)
            product = matmul(rows[q], wide, 1, 1)
            total = product if total is None else total + product
        low = total.astype(bf16)
        for r in range(8):
            out[half * 8 + r] = low[r * BLOCK : (r + 1) * BLOCK]
    copy.wait()


def compare(parts, both, state, recon, gout):
    recon_sum = jnp.sum(parts[...].astype(f32), axis=0)
    recon[...] = recon_sum.astype(bf16)
    error = recon_sum - both[1].astype(f32)
    by_lane = jnp.sum(error * error, axis=0, keepdims=True) + sparsity_weight * state[400:401]
    slope = 2.0 * error / TOK_DEV
    row = lax.broadcasted_iota(jnp.int32, (BLOCK, 128), 0)
    for k, piece in enumerate(split(by_lane)):
        slope = jnp.where(row == 108 + k, piece.astype(f32), slope)
    low = slope.astype(bf16)
    for z in range(16):
        gout[z] = low


def pull_back(gout, rows, far_out, loss, kept, out, sem, sems):
    copies = [pltpu.make_async_copy(gout, kept, sem)]
    copies[0].start()
    total = jnp.sum(gout[:, 96:112].astype(f32), axis=0)
    loss[...] = jnp.broadcast_to(jnp.sum(total[12:15], axis=0, keepdims=True), (8, 128))
    for half in range(2):
        tokens = jnp.concatenate([gout[half * 8 + r] for r in range(8)], axis=0)
        for q in range(4):
            product = matmul(tokens, rows[q], 0, 0).astype(bf16)
            for g in range(4):
                for c in range(3):
                    at = (q * 3 + c) * 32
                    out[half * 4 + g, at : at + 32] = product[
                        g * 32 : g * 32 + 32, c * 128 : c * 128 + 128
                    ]
        four = pl.ds(half * 4, 4)
        copies.append(pltpu.make_async_copy(out.at[four], far_out.at[four], sems.at[half]))
        copies[-1].start()
    for copy in copies:
        copy.wait()


def tail_of(values):
    row = lax.broadcasted_iota(jnp.int32, (16, 128), 0)
    tail = jnp.zeros((16, 128), f32)
    for k, value in enumerate(values):
        for p, piece in enumerate(split(value)):
            tail = jnp.where(row == 4 * p + k, piece.astype(f32), tail)
    return tail.astype(bf16)


def slopes_of(parts, state, loss, out):
    total = jnp.sum(parts[...].astype(f32), axis=0)
    for q in range(4):
        sums = []
        for c in range(3):
            k = q * 3 + c
            norm = state[384 + k : 385 + k]
            slope = total[k * 32 : k * 32 + 32] + (sparsity_weight / TOK_DEV) * norm
            slope = jnp.where(state[k * 32 : k * 32 + 32] > 0, slope, 0.0)
            sums.append(jnp.sum(slope, axis=0, keepdims=True))
            for yh in range(2):
                out[yh * 4 + q, c * 32 : c * 32 + 32] = slope.astype(bf16)
        tail = tail_of([*sums, loss[0:1]])
        for yh in range(2):
            out[yh * 4 + q, 96:112] = tail


def regroup(got, out):
    tail = jnp.sum(got[:, 96:112].astype(f32), axis=0)
    tail = tail[0:4] + tail[4:8] + tail[8:12]
    tail = tail_of([tail[k : k + 1] for k in range(4)])
    for x in range(4):
        for m in range(8):
            out[x, m * 96 : m * 96 + 96] = got[m, 0:96]
        out[x, 768:784] = tail


def over_tokens(blocks, values):
    total = None
    for q in range(4):
        wide = jnp.concatenate([blocks[q, 0], blocks[q, 1]], axis=1)
        column = lambda c: jnp.concatenate([values(h, q, c) for h in range(2)], axis=0)
        product = matmul(wide, jnp.concatenate([column(c) for c in range(3)], axis=1), 1, 0)
        total = product if total is None else total + product
    return total


def decoder_gradient(blocks, acts, rows, norms, source, out, total):
    def values(half, q, c):
        here = acts[q, half * 4 : half * 4 + 4, c * 32 : c * 32 + 32]
        return here.reshape(128, 128)

    total[...] = over_tokens(blocks, values)
    sums = []
    for c in range(3):
        column = acts[:, :, c * 32 : c * 32 + 32].reshape(1024, 128).astype(f32)
        sums.append(jnp.sum(column, axis=0, keepdims=True))
    pull = (sparsity_weight / TOK_DEV) * jnp.concatenate(sums, axis=1) / norms[...]
    for layer in range(LAYERS):
        for r in range(8):
            at = r * BLOCK + layer * 36
            out[layer, r * 36 : r * 36 + 36] = total[at : at + 36]
        whole = out[layer] + pull * rows[layer].astype(f32)
        out[layer] = jnp.where(source[...] <= layer, whole, 0.0)


def encoder_gradient(blocks, dpre, source, out, bias, loss, total):
    def values(half, q, c):
        parts = [
            dpre[half * 2 + g // 2, pl.ds(((g % 2) * 4 + q) * 96 + c * 32, 32)] for g in range(4)
        ]
        return jnp.concatenate(parts, axis=0)

    total[...] = over_tokens(blocks, values)
    for r in range(8):
        own = jnp.zeros((36, 384), f32)
        for layer in range(LAYERS):
            at = r * BLOCK + layer * 36
            own = own + jnp.where(source[...] == layer, total[at : at + 36], 0.0)
        out[r * 36 : r * 36 + 36] = own
    tail = jnp.sum(dpre[:, 768:784].astype(f32), axis=0)
    tail = tail[0:4] + tail[4:8] + tail[8:12]
    bias[...] = tail[0:3]
    loss[...] = jnp.sum(tail[3:4], axis=1, keepdims=True) / TOK_DEV


together = lax.optimization_barrier


def on_device(resid, target, enc_weight, enc_bias, dec_weight, source):
    to = spread()
    back = [(d, s) for s, d in to]
    source_row = source[None]

    both = jnp.stack([resid, target]).transpose(0, 2, 3, 1).reshape(2, 108, 128)
    both = jnp.pad(both, ((0, 0), (0, BLOCK - 108), (0, 0)))
    both = lax.ppermute(both, ALL, to)

    enc_t = enc_weight.T
    dec_t = dec_weight.transpose(1, 2, 0)
    dec_own, square = call(
        arrange,
        dec_t,
        source_row,
        out=[((8 * BLOCK, 384), bf16), ((1, 384), f32)],
        scratch=[pltpu.VMEM((288, 384), f32), pltpu.VMEM((8 * BLOCK, 384), f32)],
    )
    extra = jnp.stack([source.astype(bf16), *pieces(enc_bias), *pieces(square[0])])
    enc_own = jnp.concatenate([enc_t, jnp.pad(extra, ((0, 9), (0, 0)))])
    enc_quad = lax.all_gather(enc_own, QUAD)
    dec_quad = lax.all_gather(dec_own, QUAD)
    tail = enc_quad[:, 288:295].astype(f32)
    source_quad = tail[:, 0]
    bias_quad = tail[:, 1] + tail[:, 2] + tail[:, 3]
    square_quad = (tail[:, 4] + tail[:, 5] + tail[:, 6]).reshape(1536)
    x_sent, both = call(
        spread_out,
        both,
        out=[((16, BLOCK, 128), bf16), ((2, BLOCK, 128), bf16)],
        far=(1,),
        scratch=[pltpu.SemaphoreType.DMA],
    )
    x_quad = lax.all_to_all(x_sent, "z", 0, 0)
    squares = jnp.pad(square_quad.reshape(12, 128), ((0, 4), (0, 0)))
    x_quad, dec_quad, squares = together((x_quad, dec_quad, squares))
    partial, x_kept = call(
        encode,
        x_quad,
        enc_quad,
        source_quad,
        bias_quad,
        squares,
        out=[((8, 400, 128), f32), ((16, BLOCK, 128), bf16)],
        far=(1,),
        scratch=[
            pltpu.VMEM((16 * BLOCK, 128), f32),
            pltpu.VMEM((2, LAYERS, 288, 128), f32),
            pltpu.SemaphoreType.DMA,
        ],
    )
    partial = lax.all_to_all(partial, DP, 0, 0)
    state, acts = call(
        activate,
        partial,
        out=[((408, 128), f32), ((8, 384, 128), bf16)],
        far=(0,),
        scratch=[pltpu.VMEM((408, 128), f32), pltpu.SemaphoreType.DMA],
    )
    acts, x_sent = together((acts, x_kept))
    acts_quad = lax.all_to_all(acts, DP, 0, 0)

    terms, acts_kept = call(
        decode,
        dec_quad,
        acts_quad,
        out=[((16, BLOCK, 128), bf16), ((8, 384, 128), bf16)],
        far=(1,),
        scratch=[pltpu.SemaphoreType.DMA],
    )
    parts = lax.all_to_all(terms, "z", 0, 0)
    acts_every = lax.all_gather(acts_kept, QUAD)
    member = lax.axis_index(QUAD)
    acts_every = lax.dynamic_slice_in_dim(acts_every, member * 96, 96, 2)
    recon, gout = call(
        compare,
        parts,
        both,
        state,
        out=[((BLOCK, 128), bf16), ((16, BLOCK, 128), bf16)],
    )
    x_every = lax.all_gather(x_sent.reshape(2, 8 * BLOCK, 128), QUAD)
    gout, x_every = together((gout, x_every))
    gout_all = lax.all_to_all(gout, "z", 0, 0)

    slopes, loss_z, gout_kept = call(
        pull_back,
        gout_all,
        dec_quad,
        out=[((8, 384, 128), bf16), ((8, 128), f32), ((16, BLOCK, 128), bf16)],
        far=(0, 2),
        scratch=[
            pltpu.VMEM((8, 384, 128), bf16),
            pltpu.SemaphoreType.DMA,
            pltpu.SemaphoreType.DMA((2,)),
        ],
    )
    gout_every = lax.all_gather(gout_kept.reshape(2, 8 * BLOCK, 128), QUAD)
    slopes = lax.all_to_all(slopes, DP, 0, 0)
    (sent,) = call(slopes_of, slopes, state, loss_z, out=[((8, 112, 128), bf16)])
    got = lax.all_to_all(sent, PLANE, 0, 0)
    (sent,) = call(regroup, got, out=[((4, 784, 128), bf16)])
    got = lax.all_to_all(sent, "x", 0, 0)

    total = pltpu.VMEM((8 * BLOCK, 384), f32)
    own_norms = lax.dynamic_index_in_dim(state[384:396].reshape(4, 384), member, 0, True)
    (dec_grad,) = call(
        decoder_gradient,
        gout_every,
        acts_every,
        dec_t,
        own_norms,
        source_row,
        out=[((LAYERS, 288, 384), f32)],
        scratch=[total],
    )
    got, dec_grad = together((got, dec_grad))
    enc_grad, bias_grad, loss = call(
        encoder_gradient,
        x_every,
        got,
        source_row,
        out=[((288, 384), f32), ((3, 128), f32), ((1, 1), f32)],
        scratch=[total],
    )
    recon = lax.ppermute(recon, ALL, back)
    recon, enc_grad = together((recon, enc_grad))
    recon = recon[:108].reshape(3, 36, 128).transpose(2, 0, 1)
    return (loss[0, 0], recon, enc_grad.T, bias_grad.reshape(384), dec_grad.transpose(2, 0, 1))


def solution(mesh):
    fine = Mesh(np.asarray(mesh.devices).reshape(SIZES), ALL)
    in_specs = (
        P(DP, None, LATENT),
        P(DP, None, LATENT),
        P(LATENT, DP),
        P(LATENT),
        P(LATENT, None, DP),
        P(LATENT),
    )
    out_specs = (
        P(),
        P(DP, None, LATENT),
        P(LATENT, DP),
        P(LATENT),
        P(LATENT, None, DP),
    )
    return jax.shard_map(
        on_device, mesh=fine, in_specs=in_specs, out_specs=out_specs, check_vma=False
    )
```
